256 devices in a mesh: row: 32 (over x, z), feat: 8 (over y, core).
Axes of the slice: x: 4, y: 4, z: 8, core: 2. Of those that a mesh axis runs over, the one named last changes fastest.
Arguments:
- candidates: bfloat16 [2048, 16384], P('row', 'feat'), may hold values from -48 to 48, as said below
- inv_factor: bfloat16 [16384, 16384], P('row', 'feat'), may hold values from -1.5 to 1.5, as said below
- weights: float32 [2048], P('row'), may hold values from 0.01 to 0.1
- strata: int32 [2048], P('row'), may hold values from 0 to 63, never falling along the last dimension, each value on 1 to 256 neighbouring positions
Outputs:
- new_weight: float32 [2048], P('row')
- leverage: float32 [2048], P('row')
- information: float32 [16384, 16384], P('row', 'feat')
The draws below stay inside these ranges and needn't reach their ends.
Inputs may be any that keep to these rules, and one draw needn't show every extreme that they name: `candidates`: row scales and column scales differ. `inv_factor`: zero above the diagonal, positive on the diagonal.
All inputs are finite; a program needn't handle non-finite values.
Results may differ from the reference program's by a relative error of at most 0.0029.
Values may be sent and summed in bfloat16 or wider, within the bound.
A program may use at most 64 MiB of HBM per device.

```python
import math
import jax
import jax.numpy as jnp
import numpy as np
from jax import lax

FEATURES = 16384
ROWS = 2048
STRATA = 64
MOST = 256


def draw_candidates(key, part):
    key_row, key_col, key_base = jax.random.split(key, 3)
    rising = jnp.exp(math.log(3.0) * jnp.arange(ROWS, dtype=jnp.float32) / ROWS)
    row_scale = rising * jnp.exp(jax.random.uniform(key_row, (ROWS,), jnp.float32, math.log(0.5), math.log(2.0)))
    col_scale = jnp.exp(jax.random.uniform(key_col, (FEATURES,), jnp.float32, math.log(0.5), math.log(2.0)))
    base_draw = jnp.clip(jax.random.normal(key_base, (ROWS, FEATURES), jnp.float32), -4.0, 4.0)
    return (row_scale[:, None] * col_scale[None, :] * base_draw).astype(jnp.bfloat16)


def draw_inv_factor(key, part):
    key_noise, key_diag = jax.random.split(key, 2)
    indices = jnp.arange(FEATURES, dtype=jnp.int32)
    spread = 0.8 / math.sqrt(FEATURES)
    noise_part = jnp.clip(jax.random.normal(key_noise, (FEATURES, FEATURES), jnp.float32), -4.0, 4.0) * spread
    diagonal = jnp.exp(jax.random.uniform(key_diag, (FEATURES,), jnp.float32, math.log(0.7), math.log(1.4)))
    below_diag = indices[:, None] > indices[None, :]
    on_diag = indices[:, None] == indices[None, :]
    filled = jnp.where(below_diag, noise_part, 0.0) + jnp.where(on_diag, diagonal[:, None], 0.0)
    return filled.astype(jnp.bfloat16)


def shard_levels(own_key, shape, cuts, least, top_value):
    factor_of, own = 1.0, jax.random.fold_in(own_key, 6)
    for position, shards_of in cuts:
        heights = jnp.exp(jax.random.uniform(jax.random.fold_in(own, position), (shards_of,), jnp.float32, least / len(cuts), top_value / len(cuts)))
        factor_of = factor_of * jnp.repeat(heights, shape[position] // shards_of).reshape([-1 if axis == position else 1 for axis in range(len(shape))])
    return factor_of


def split_up(number_of, total, limit, skew):
    portions = [(1 << 20) // math.isqrt(grade ** skew) + 1 for grade in range(2, number_of + 1)]
    rest, holding = total - limit - (number_of - 1), [1] * (number_of - 1)
    while rest > 0:
        movable = [i for i in range(number_of - 1) if holding[i] < limit]
        whole, remaining = sum([portions[i] for i in movable]), rest
        for i in movable:
            extra = min(limit - holding[i], max(1, remaining * portions[i] // whole), rest)
            holding[i] = holding[i] + extra
            rest = rest - extra
    return np.array([limit] + holding)


def uneven(key, number_of, total, bound, slope):
    if number_of == 2:
        one = jax.random.randint(key, (), max(1, total - bound), min(bound, total - 1) + 1)
        return jnp.stack([one, total - one])
    tallies = jnp.asarray(split_up(number_of, total, bound, slope), jnp.int32)
    twos = (number_of - 1) // 2
    source_of, sink = tallies[1:1 + 2 * twos:2], tallies[2:2 + 2 * twos:2]
    room = jnp.minimum(source_of - 1, bound - sink)
    moved = jax.random.randint(jax.random.fold_in(key, 1), (twos,), 0, 1 << 20) % (room + 1)
    tallies = tallies.at[1:1 + 2 * twos:2].set(source_of - moved).at[2:2 + 2 * twos:2].set(sink + moved)
    return tallies[jax.random.permutation(jax.random.fold_in(key, 2), number_of)]


def setup_inputs(seed: int = 0) -> dict:
    key_list = jax.random.split(jax.random.key(seed), 5)
    candidates = draw_candidates(jax.random.fold_in(key_list[4], 71), 0)
    inv_factor = draw_inv_factor(jax.random.fold_in(key_list[4], 71), 0)
    weights = jnp.clip(jnp.exp(math.log(0.1) - 2.3025851 * jax.random.uniform(key_list[2], (ROWS,), jnp.float32) ** shard_levels(key_list[2], (ROWS,), ((0, 32),), -0.2, 0.2)), 0.01, 0.1)
    strata = jnp.searchsorted(jnp.cumsum(uneven(key_list[3], STRATA, ROWS, MOST, 2)), jnp.arange(ROWS), side="right").astype(jnp.int32)
    return dict(candidates=candidates, inv_factor=inv_factor, weights=weights, strata=strata)


def reference(candidates, inv_factor, weights, strata):
    whitened = lax.dot_general(candidates, inv_factor, (((1,), (1,)), ((), ())), preferred_element_type=jnp.float32)
    raw_leverage = jnp.sum(whitened * whitened, axis=1)
    leverage = raw_leverage / FEATURES
    products = weights * raw_leverage
    stratum_product = jax.ops.segment_sum(products, strata, num_segments=STRATA)
    stratum_mass = jax.ops.segment_sum(weights, strata, num_segments=STRATA)
    stratum_ratio = stratum_mass / stratum_product
    new_weight = products * stratum_ratio[strata]
    weight_step = new_weight - weights
    scaled = (weight_step[:, None] * candidates.astype(jnp.float32)).astype(jnp.bfloat16)
    information = lax.dot_general(candidates, scaled, (((0,), (0,)), ((), ())), preferred_element_type=jnp.float32)
    return (new_weight, leverage, information)
```

```python
import functools

import jax
import jax.numpy as jnp
from jax import lax
from jax.experimental import pallas as pl
from jax.experimental.pallas import tpu as pltpu
from jax.sharding import PartitionSpec as P

MESH = pl.DeviceIdType.MESH
NX, NY, NZ, NC = 4, 4, 8, 2
STRATA = 64
CUT = 768
OFFSETS = (0, 1, -1, 2, -2, 3, -3, 4)


def gather_kernel(
    cand, fac, wt,
    G, S, nw_ref, lev_ref,
    F, Ci, pb, px, ysb, ysr, V, wx, wz0, wz, lx, lz0, lz, lt0, lt,
    loc_sem, gs, gr, ws, wr, pxs, pxr, yss, ysrs, cs, cr, ls, lr,
):
    features = NY * NC * cand.shape[1]
    row, feat = lax.axis_index("row"), lax.axis_index("feat")
    x, z = row // NZ, row % NZ
    y, c = feat // NC, feat % NC

    def xdev(d):
        return (lax.rem(x + d + NX, NX) * NZ + z, feat)

    def zdev(d):
        return (x * NZ + lax.rem(z + d + NZ, NZ), feat)

    def fdev(dy, dc):
        return (row, lax.rem(y + dy, NY) * NC + lax.rem(c + dc, NC))

    fcopies = [(dy, dc) for dy in range(NY) for dc in range(NC) if (dy, dc) != (0, 0)]

    def xx(d):
        return lax.rem(x + d + NX, NX)

    def zz(d):
        return lax.rem(z + d + NZ, NZ)

    fcopy = pltpu.make_async_copy(fac, F, loc_sem.at[0])
    fcopy.start()
    mine = pltpu.make_async_copy(cand, G.at[x // 2, z, x % 2], loc_sem.at[1])
    mine.start()

    barrier = pltpu.get_barrier_semaphore()
    peers = (
        [xdev(d) for d in range(1, NX)] + [zdev(d) for d in range(1, NZ)] + [fdev(*d) for d in fcopies]
    )
    for dev in peers:
        pl.semaphore_signal(barrier, inc=1, device_id=dev, device_id_type=MESH)
    mine.wait()
    pl.semaphore_wait(barrier, len(peers))

    pending = []

    def remote(src, dst, ssem, rsem, dev):
        cp = pltpu.make_async_remote_copy(
            src_ref=src, dst_ref=dst, send_sem=ssem, recv_sem=rsem, device_id=dev, device_id_type=MESH
        )
        cp.start()
        pending.append(cp)
        return cp

    count = [0]

    def gsend(view, dev):
        k = count[0]
        count[0] += 1
        return remote(view, view, gs.at[k], gr.at[k], dev)

    cols_a, cols_b = pl.ds(0, CUT), pl.ds(CUT, cand.shape[1] - CUT)
    rows_dev = cand.shape[0]
    half = rows_dev // 2
    SIGNS = (1, -1)

    def half_of(s):
        return pl.ds(0 if s > 0 else half, half)

    def chunk(xp, zp, cols, rows=None):
        if rows is None:
            rows = pl.ds(0, rows_dev)
        return G.at[xp // 2, zp, xp % 2, rows, cols]

    def plane(cp, zp):
        return G.at[cp, zp, :, :, cols_a]

    XA1, XA2, ZB, ZA, XB, XH = {}, {}, {}, {}, {}, {}

    def start_xb(o):
        for s in SIGNS:
            XB[o, s] = gsend(chunk(x, zz(o), cols_b), xdev(s))

    def forward_xb(o):
        for s in SIGNS:
            XB[o, s].wait_recv()
            XH[o, s] = gsend(chunk(xx(-s), zz(o), cols_b, half_of(s)), xdev(s))

    def finish_xh(o):
        for s in SIGNS:
            XH[o, s].wait_recv()

    def forward_zb(d):
        for s in SIGNS:
            ZB[d, s].wait_recv()
            if d < 3:
                ZB[d + 1, s] = gsend(chunk(x, zz(-s * d), cols_b), zdev(s))
            elif d == 3:
                ZB[d + 1, s] = gsend(chunk(x, zz(-s * d), cols_b, half_of(s)), zdev(s))

    def forward_za(d):
        for cp in range(2):
            for s in SIGNS:
                if (d, s, cp) not in ZA:
                    continue
                ZA[d, s, cp].wait_recv()
                if d < 3 or (d == 3 and cp == (0 if s > 0 else 1)):
                    ZA[d + 1, s, cp] = gsend(plane(cp, zz(-s * d)), zdev(s))

    def product(o):
        zp = zz(o)
        a = G[:, zp].reshape(NX * rows_dev, cand.shape[1])
        for n in range(2):
            rows = pl.ds(n * 256, 256)
            p = lax.dot_general(
                F[rows, :], a, (((1,), (1,)), ((), ())), preferred_element_type=jnp.float32
            ).astype(jnp.bfloat16)
            pb[zp, 0, rows, :] = p[:, :128]
            pb[zp, 1, rows, :] = p[:, 128:]

    PX, YS = {}, {}

    def send_half(o):
        i = OFFSETS.index(o)
        zp = zz(o)
        PX[o] = remote(pb.at[zp, 1 - c], px.at[zp], pxs.at[i], pxr.at[i], fdev(0, 1))

    def send_quarters(o):
        i = OFFSETS.index(o)
        zp = zz(o)
        PX[o].wait_recv()
        q = pb[zp, c].astype(jnp.float32) + px[zp].astype(jnp.float32)
        ysb[zp] = q.astype(jnp.bfloat16).reshape(NY, 128, 128)
        for d in range(1, NY):
            yp = lax.rem(y + d, NY)
            YS[o, d] = remote(
                ysb.at[zp, yp], ysr.at[zp, d], yss.at[i * 3 + d - 1], ysrs.at[i * 3 + d - 1], fdev(d, 0)
            )

    def squares(o):
        zp = zz(o)
        total = ysb[zp, y].astype(jnp.float32)
        for d in range(1, NY):
            YS[o, d].wait_recv()
            total = total + ysr[zp, d].astype(jnp.float32)
        V[pl.ds(zp, 1), :] = jnp.sum(total * total, axis=0, keepdims=True)

    block = Ci.shape[-1]
    col0 = pl.multiple_of((z % 4) * block, block)
    croot = z // 4
    dy = lax.rem(y - x + NY, NY)
    on_core = c == croot
    is_root = jnp.logical_and(dy == 0, on_core)

    def ci_copy(o, slot, src, dev):
        i = OFFSETS.index(o)
        return pltpu.make_async_remote_copy(
            src_ref=src, dst_ref=Ci.at[:, zz(o)], send_sem=cs.at[i * 3 + slot], recv_sem=cr.at[i],
            device_id=dev, device_id_type=MESH,
        )

    def ci_source(o):
        return G.at[:, zz(o), :, :, pl.ds(col0, block)]

    def ci_root(o):
        @pl.when(is_root)
        def _():
            src = ci_source(o)
            ci_copy(o, 0, src, fdev(1, 0)).start()
            ci_copy(o, 1, src, fdev(3, 0)).start()
            ci_copy(o, 2, src, fdev(0, 1)).start()
            own = pltpu.make_async_copy(src, Ci.at[:, zz(o)], cr.at[OFFSETS.index(o)])
            own.start()
            own.wait()

    def relays(o):
        i = OFFSETS.index(o)
        src = Ci.at[:, zz(o)]
        far = jnp.logical_and(on_core, dy == (1 if i % 2 == 0 else 3))
        far_dev = fdev(1 if i % 2 == 0 else 3, 0)
        near = jnp.logical_and(on_core, dy != 0)
        return src, far, far_dev, near

    def ci_step(o):
        @pl.when(jnp.logical_not(is_root))
        def _():
            ci_copy(o, 0, Ci.at[:, zz(o)], fdev(0, 1)).wait_recv()

        src, far, far_dev, near = relays(o)

        @pl.when(far)
        def _():
            ci_copy(o, 0, src, far_dev).start()

        @pl.when(near)
        def _():
            ci_copy(o, 2, src, fdev(0, 1)).start()

        for cp in range(2):
            t = Ci[cp, zz(o)].reshape(128, block)
            S[:, pl.ds(pl.multiple_of((cp * NZ + zz(o)) * 128, 128), 128)] = t.T

    def ci_finish(o):
        src, far, far_dev, near = relays(o)

        @pl.when(is_root)
        def _():
            for slot in range(3):
                ci_copy(o, slot, ci_source(o), fdev(0, 1)).wait_send()

        @pl.when(far)
        def _():
            ci_copy(o, 0, src, far_dev).wait_send()

        @pl.when(near)
        def _():
            ci_copy(o, 2, src, fdev(0, 1)).wait_send()

    for s in SIGNS:
        XA1[s] = gsend(chunk(x, z, cols_a), xdev(s))
    for s in SIGNS:
        ZB[1, s] = gsend(chunk(x, z, cols_b), zdev(s))
    WX = [remote(wt, wx.at[d], ws.at[d - 1], wr.at[d - 1], xdev(d)) for d in range(1, NX)]
    start_xb(0)
    for s in SIGNS:
        XA1[s].wait_recv()
        XA2[s] = gsend(chunk(xx(-s), z, cols_a, half_of(s)), xdev(s))
    forward_zb(1)
    start_xb(1)
    start_xb(-1)
    forward_xb(0)
    for s in SIGNS:
        XA2[s].wait_recv()
    for cp in range(2):
        for s in SIGNS:
            ZA[1, s, cp] = gsend(plane(cp, z), zdev(s))
    total = wt[...]
    for d in range(1, NX):
        WX[d - 1].wait_recv()
        total = total + wx[d]
    wz0[...] = total
    WZ = [remote(wz0, wz.at[d], ws.at[d + 2], wr.at[d + 2], zdev(d)) for d in range(1, NZ)]
    fcopy.wait()

    forward_zb(2)
    start_xb(2)
    start_xb(-2)
    forward_xb(1)
    forward_xb(-1)
    finish_xh(0)
    product(0)
    send_half(0)
    ci_root(0)
    forward_zb(3)
    start_xb(3)
    start_xb(-3)
    forward_za(1)
    send_quarters(0)
    finish_xh(1)
    finish_xh(-1)
    product(1)
    send_half(1)
    product(-1)
    send_half(-1)
    ci_root(1)
    ci_root(-1)
    ci_step(0)
    forward_xb(2)
    forward_xb(-2)
    forward_zb(4)
    start_xb(4)
    squares(0)
    send_quarters(1)
    send_quarters(-1)
    forward_za(2)
    finish_xh(2)
    finish_xh(-2)
    product(2)
    send_half(2)
    product(-2)
    send_half(-2)
    ci_root(2)
    ci_root(-2)
    ci_step(1)
    ci_step(-1)
    forward_xb(3)
    forward_xb(-3)
    squares(1)
    squares(-1)
    send_quarters(2)
    send_quarters(-2)
    total = wz0[...]
    for d in range(1, NZ):
        WZ[d - 1].wait_recv()
        total = total + wz[d]
    wz0_all = total
    forward_za(3)
    finish_xh(3)
    finish_xh(-3)
    product(3)
    send_half(3)
    product(-3)
    send_half(-3)
    forward_xb(4)
    ci_root(3)
    ci_root(-3)
    squares(2)
    squares(-2)
    send_quarters(3)
    send_quarters(-3)
    ci_step(2)
    ci_step(-2)
    forward_za(4)
    finish_xh(4)
    product(4)
    send_half(4)
    ci_root(4)
    squares(3)
    squares(-3)
    send_quarters(4)
    squares(4)

    v = V[...]
    lx[0] = v
    LX = [remote(lx.at[0], lx.at[d], ls.at[d - 1], lr.at[d - 1], xdev(d)) for d in range(1, NX)]
    ci_step(3)
    ci_step(-3)
    for cp in LX:
        cp.wait_recv()
    lz0[...] = (lx[0] + lx[1]) + (lx[2] + lx[3])
    LZ = [remote(lz0, lz.at[d], ls.at[d + 2], lr.at[d + 2], zdev(d)) for d in range(1, NZ)]
    ci_step(4)
    v = lz0[...]
    for d in range(1, NZ):
        LZ[d - 1].wait_recv()
        v = v + lz[d]
    lt0[...] = v
    LT = [
        remote(lt0, lt.at[k], ls.at[k + 9], lr.at[k + 9], fdev(*d)) for k, d in enumerate(fcopies, 1)
    ]
    weights = [wz0_all[0], wz0_all[1]]
    labels = [wz0_all[2], wz0_all[3]]
    ids = lax.broadcasted_iota(jnp.int32, (STRATA, 128), 0).astype(jnp.float32)

    def over_strata(tiles):
        acc = jnp.zeros((STRATA, 128), jnp.float32)
        for cp in range(2):
            for zp in range(NZ):
                acc = acc + jnp.where(labels[cp][zp : zp + 1, :] == ids, tiles[cp][zp : zp + 1, :], 0.0)
        return jnp.sum(acc, axis=1, keepdims=True)

    mass = over_strata(weights)
    same, other = lt0[...], None
    for k, (dyk, dck) in enumerate(fcopies, 1):
        LT[k - 1].wait_recv()
        if dck == 0:
            same = same + lt[k]
        else:
            other = lt[k] if other is None else other + lt[k]
    first = c == 0
    raw = [jnp.where(first, same, other), jnp.where(first, other, same)]
    products = [weights[cp] * raw[cp] for cp in range(2)]
    ratio = mass / over_strata(products)
    for cp in range(2):
        rows = [
            jnp.sum(jnp.where(labels[cp][zp : zp + 1, :] == ids, ratio, 0.0), axis=0, keepdims=True)
            for zp in range(NZ)
        ]
        row_ratio = jnp.concatenate(rows, axis=0)
        new_weight = products[cp] * row_ratio
        nw_ref[cp] = new_weight
        lev_ref[cp] = raw[cp] / features
        step = new_weight - weights[cp]
        for zp in range(NZ):
            cols = pl.ds((cp * NZ + zp) * 128, 128)
            S[:, cols] = (S[:, cols].astype(jnp.float32) * step[zp : zp + 1, :]).astype(jnp.bfloat16)

    for cp in pending:
        cp.wait_send()
    for o in OFFSETS:
        ci_finish(o)


def gather(cand, fac, wt):
    rows_dev, feat_block = cand.shape
    row_block = fac.shape[0]
    bf, f32 = jnp.bfloat16, jnp.float32
    vmem = pl.BlockSpec(memory_space=pltpu.VMEM)
    anys = pl.BlockSpec(memory_space=pl.ANY)
    dma = pltpu.SemaphoreType.DMA
    return pl.pallas_call(
        gather_kernel,
        out_shape=(
            pltpu.VMEM((2, NZ, 2, rows_dev, feat_block), bf),
            pltpu.VMEM((row_block, NX * NZ * rows_dev), bf),
            jax.ShapeDtypeStruct((2, NZ, 128), f32),
            jax.ShapeDtypeStruct((2, NZ, 128), f32),
        ),
        in_specs=[anys, anys, vmem],
        out_specs=(vmem, vmem, vmem, vmem),
        scratch_shapes=[
            pltpu.VMEM(fac.shape, bf),
            pltpu.VMEM((2, NZ, 2, rows_dev, row_block), bf),
            pltpu.VMEM((NZ, 2, row_block, 128), bf),
            pltpu.VMEM((NZ, row_block, 128), bf),
            pltpu.VMEM((NZ, NY, 128, 128), bf),
            pltpu.VMEM((NZ, NY, 128, 128), bf),
            pltpu.VMEM((NZ, 128), f32),
            pltpu.VMEM((NX, 4, NZ, 128), f32),
            pltpu.VMEM((4, NZ, 128), f32),
            pltpu.VMEM((NZ, 4, NZ, 128), f32),
            pltpu.VMEM((NX, NZ, 128), f32),
            pltpu.VMEM((NZ, 128), f32),
            pltpu.VMEM((NZ, NZ, 128), f32),
            pltpu.VMEM((NZ, 128), f32),
            pltpu.VMEM((NZ, NZ, 128), f32),
            dma((2,)),
            dma((58,)),
            dma((58,)),
            dma((10,)),
            dma((10,)),
            dma((8,)),
            dma((8,)),
            dma((24,)),
            dma((24,)),
            dma((24,)),
            dma((8,)),
            dma((17,)),
            dma((17,)),
        ],
        compiler_params=pltpu.CompilerParams(
            collective_id=0, has_side_effects=True, vmem_limit_bytes=40 * 1024 * 1024
        ),
    )(cand, fac, wt)


def increment_kernel(s_ref, g_ref, o_ref):
    j = pl.program_id(0)
    n = o_ref.shape[1]
    cols = pl.ds(pl.multiple_of(j * n, n), n)
    o_ref[...] = jnp.dot(s_ref[...], g_ref[:, cols], preferred_element_type=jnp.float32)


def increment(s, g):
    rows, depth = s.shape
    columns = g.shape[1]
    width = 256
    vmem = pl.BlockSpec(memory_space=pltpu.VMEM)
    return pl.pallas_call(
        increment_kernel,
        grid=(columns // width,),
        out_shape=jax.ShapeDtypeStruct((rows, columns), jnp.float32),
        in_specs=[vmem, vmem],
        out_specs=pl.BlockSpec((rows, width), lambda j: (0, j)),
        compiler_params=pltpu.CompilerParams(vmem_limit_bytes=24 * 1024 * 1024),
    )(s, g)


def per_device(candidates, inv_factor, weights, strata):
    row = lax.axis_index("row")
    x, z = row // NZ, row % NZ
    at = jnp.logical_and(
        jnp.arange(2)[:, None, None] == x // 2,
        jnp.logical_and(
            jnp.arange(NZ)[None, :, None] == z, jnp.arange(128)[None, None, :] // 64 == x % 2
        ),
    )
    pair = jnp.stack([jnp.tile(weights, 2), jnp.tile(strata.astype(jnp.float32), 2)])
    wt = jnp.where(at[None], pair[:, None, None, :], 0.0).reshape(4, NZ, 128)
    g, s, nw, lev = gather(candidates, inv_factor, wt)
    information = increment(s, g.reshape(-1, g.shape[-1]))
    start = (x // 2, z, (x % 2) * 64)
    new_weight = lax.dynamic_slice(nw, start, (1, 1, 64)).reshape(64)
    leverage = lax.dynamic_slice(lev, start, (1, 1, 64)).reshape(64)
    return (new_weight, leverage, information)


def solution(mesh):
    in_specs = (P("row", "feat"), P("row", "feat"), P("row"), P("row"))
    out_specs = (P("row"), P("row"), P("row", "feat"))
    return jax.shard_map(
        per_device, mesh=mesh, in_specs=in_specs, out_specs=out_specs, check_vma=False
    )
```

```python
import functools

import jax
import jax.numpy as jnp
from jax import lax
from jax.experimental import pallas as pl
from jax.experimental.pallas import tpu as pltpu
from jax.sharding import PartitionSpec as P

MESH = pl.DeviceIdType.MESH
NX, NY, NZ, NC = 4, 4, 8, 2
STRATA = 64
CUT = 768
OFFSETS = (0, 1, -1, 2, -2, 3, -3, 4)


def gather_kernel(
    cand, fac, w_hbm, st_hbm,
    G, S, nw_ref, lev_ref,
    w_ref, st_ref, twice, wt, F, Ci, pb, px, ysb, ysr, V, wx, wz0, wz, lx, lz0, lz, lt0, lt,
    loc_sem, gs, gr, ws, wr, pxs, pxr, yss, ysrs, cs, cr, ls, lr,
):
    features = NY * NC * cand.shape[1]
    row, feat = lax.axis_index("row"), lax.axis_index("feat")
    x, z = row // NZ, row % NZ
    y, c = feat // NC, feat % NC

    def xdev(d):
        return (lax.rem(x + d + NX, NX) * NZ + z, feat)

    def zdev(d):
        return (x * NZ + lax.rem(z + d + NZ, NZ), feat)

    def fdev(dy, dc):
        return (row, lax.rem(y + dy, NY) * NC + lax.rem(c + dc, NC))

    fcopies = [(dy, dc) for dy in range(NY) for dc in range(NC) if (dy, dc) != (0, 0)]

    def xx(d):
        return lax.rem(x + d + NX, NX)

    def zz(d):
        return lax.rem(z + d + NZ, NZ)

    fcopy = pltpu.make_async_copy(fac, F, loc_sem.at[0])
    smalls = [
        pltpu.make_async_copy(w_hbm, w_ref, loc_sem.at[2]),
        pltpu.make_async_copy(st_hbm, st_ref, loc_sem.at[3]),
    ]
    mine = pltpu.make_async_copy(cand, G.at[x // 2, z, x % 2], loc_sem.at[1])
    mine.start()
    for cp in smalls:
        cp.start()
    fcopy.start()

    barrier = pltpu.get_barrier_semaphore()
    peers = (
        [xdev(d) for d in range(1, NX)] + [zdev(d) for d in range(1, NZ)] + [fdev(*d) for d in fcopies]
    )
    for dev in peers:
        pl.semaphore_signal(barrier, inc=1, device_id=dev, device_id_type=MESH)
    for cp in smalls:
        cp.wait()
    twice[0:1, 0:64] = w_ref[...]
    twice[0:1, 64:128] = w_ref[...]
    twice[1:2, 0:64] = st_ref[...].astype(jnp.float32)
    twice[1:2, 64:128] = st_ref[...].astype(jnp.float32)
    sub = lax.broadcasted_iota(jnp.int32, (NZ, 128), 0)
    lane = lax.broadcasted_iota(jnp.int32, (NZ, 128), 1)
    here = jnp.logical_and(sub == z, lane // 64 == x % 2)
    for k in range(2):
        placed = jnp.where(here, twice[k : k + 1, :], 0.0)
        for cp in range(2):
            wt[2 * k + cp] = jnp.where(x // 2 == cp, placed, 0.0)

    mine.wait()
    pl.semaphore_wait(barrier, len(peers))

    pending = []

    def remote(src, dst, ssem, rsem, dev):
        cp = pltpu.make_async_remote_copy(
            src_ref=src, dst_ref=dst, send_sem=ssem, recv_sem=rsem, device_id=dev, device_id_type=MESH
        )
        cp.start()
        pending.append(cp)
        return cp

    count = [0]

    def gsend(view, dev):
        k = count[0]
        count[0] += 1
        return remote(view, view, gs.at[k], gr.at[k], dev)

    cols_a, cols_b = pl.ds(0, CUT), pl.ds(CUT, cand.shape[1] - CUT)
    rows_dev = cand.shape[0]
    half = rows_dev // 2
    SIGNS = (1, -1)

    def half_of(s):
        return pl.ds(0 if s > 0 else half, half)

    def chunk(xp, zp, cols, rows=None):
        if rows is None:
            rows = pl.ds(0, rows_dev)
        return G.at[xp // 2, zp, xp % 2, rows, cols]

    def plane(cp, zp):
        return G.at[cp, zp, :, :, cols_a]

    XA1, XA2, ZB, ZA, XB, XH = {}, {}, {}, {}, {}, {}

    def start_xb(o):
        for s in SIGNS:
            XB[o, s] = gsend(chunk(x, zz(o), cols_b), xdev(s))

    def forward_xb(o):
        for s in SIGNS:
            XB[o, s].wait_recv()
            XH[o, s] = gsend(chunk(xx(-s), zz(o), cols_b, half_of(s)), xdev(s))

    def finish_xh(o):
        for s in SIGNS:
            XH[o, s].wait_recv()

    def forward_zb(d):
        for s in SIGNS:
            ZB[d, s].wait_recv()
            if d < 3:
                ZB[d + 1, s] = gsend(chunk(x, zz(-s * d), cols_b), zdev(s))
            elif d == 3:
                ZB[d + 1, s] = gsend(chunk(x, zz(-s * d), cols_b, half_of(s)), zdev(s))

    def forward_za(d):
        for cp in range(2):
            for s in SIGNS:
                if (d, s, cp) not in ZA:
                    continue
                ZA[d, s, cp].wait_recv()
                if d < 3 or (d == 3 and cp == (0 if s > 0 else 1)):
                    ZA[d + 1, s, cp] = gsend(plane(cp, zz(-s * d)), zdev(s))

    def product(o):
        zp = zz(o)
        a = G[:, zp].reshape(NX * rows_dev, cand.shape[1])
        for n in range(2):
            rows = pl.ds(n * 256, 256)
            p = lax.dot_general(
                F[rows, :], a, (((1,), (1,)), ((), ())), preferred_element_type=jnp.float32
            ).astype(jnp.bfloat16)
            pb[zp, 0, rows, :] = p[:, :128]
            pb[zp, 1, rows, :] = p[:, 128:]

    PX, YS = {}, {}

    def send_half(o):
        i = OFFSETS.index(o)
        zp = zz(o)
        PX[o] = remote(pb.at[zp, 1 - c], px.at[zp], pxs.at[i], pxr.at[i], fdev(0, 1))

    def send_quarters(o):
        i = OFFSETS.index(o)
        zp = zz(o)
        PX[o].wait_recv()
        q = pb[zp, c].astype(jnp.float32) + px[zp].astype(jnp.float32)
        ysb[zp] = q.astype(jnp.bfloat16).reshape(NY, 128, 128)
        for d in range(1, NY):
            yp = lax.rem(y + d, NY)
            YS[o, d] = remote(
                ysb.at[zp, yp], ysr.at[zp, d], yss.at[i * 3 + d - 1], ysrs.at[i * 3 + d - 1], fdev(d, 0)
            )

    def squares(o):
        zp = zz(o)
        total = ysb[zp, y].astype(jnp.float32)
        for d in range(1, NY):
            YS[o, d].wait_recv()
            total = total + ysr[zp, d].astype(jnp.float32)
        V[pl.ds(zp, 1), :] = jnp.sum(total * total, axis=0, keepdims=True)

    block = Ci.shape[-1]
    col0 = pl.multiple_of((z % 4) * block, block)
    croot = z // 4
    dy = lax.rem(y - x + NY, NY)
    on_core = c == croot
    is_root = jnp.logical_and(dy == 0, on_core)

    def ci_copy(o, slot, src, dev):
        i = OFFSETS.index(o)
        return pltpu.make_async_remote_copy(
            src_ref=src, dst_ref=Ci.at[:, zz(o)], send_sem=cs.at[i * 3 + slot], recv_sem=cr.at[i],
            device_id=dev, device_id_type=MESH,
        )

    def ci_source(o):
        return G.at[:, zz(o), :, :, pl.ds(col0, block)]

    def ci_root(o):
        @pl.when(is_root)
        def _():
            src = ci_source(o)
            ci_copy(o, 0, src, fdev(1, 0)).start()
            ci_copy(o, 1, src, fdev(3, 0)).start()
            ci_copy(o, 2, src, fdev(0, 1)).start()
            own = pltpu.make_async_copy(src, Ci.at[:, zz(o)], cr.at[OFFSETS.index(o)])
            own.start()
            own.wait()

    def ci_wait(o):
        ci_copy(o, 0, Ci.at[:, zz(o)], fdev(0, 1)).wait_recv()

    def ci_near(o):
        i = OFFSETS.index(o)
        for d in (1, 3):
            @pl.when(jnp.logical_and(on_core, dy == d))
            def _():
                ci_wait(o)
                if d == (1 if i % 2 == 0 else 3):
                    ci_copy(o, 0, Ci.at[:, zz(o)], fdev(d, 0)).start()
                ci_copy(o, 2, Ci.at[:, zz(o)], fdev(0, 1)).start()

    def ci_far(o):
        @pl.when(jnp.logical_and(on_core, dy == 2))
        def _():
            ci_wait(o)
            ci_copy(o, 2, Ci.at[:, zz(o)], fdev(0, 1)).start()

    def ci_last(o):
        @pl.when(jnp.logical_not(on_core))
        def _():
            ci_wait(o)

        for cp in range(2):
            t = Ci[cp, zz(o)].reshape(128, block)
            S[:, pl.ds(pl.multiple_of((cp * NZ + zz(o)) * 128, 128), 128)] = t.T

    def ci_finish(o):
        i = OFFSETS.index(o)

        @pl.when(is_root)
        def _():
            for slot in range(3):
                ci_copy(o, slot, ci_source(o), fdev(0, 1)).wait_send()

        for d in (1, 2, 3):
            @pl.when(jnp.logical_and(on_core, dy == d))
            def _():
                if d == (1 if i % 2 == 0 else 3):
                    ci_copy(o, 0, Ci.at[:, zz(o)], fdev(0, 1)).wait_send()
                ci_copy(o, 2, Ci.at[:, zz(o)], fdev(0, 1)).wait_send()

    for s in SIGNS:
        XA1[s] = gsend(chunk(x, z, cols_a), xdev(s))
    for s in SIGNS:
        ZB[1, s] = gsend(chunk(x, z, cols_b), zdev(s))
    WX = [remote(wt, wx.at[d], ws.at[d - 1], wr.at[d - 1], xdev(d)) for d in range(1, NX)]
    start_xb(0)
    for s in SIGNS:
        XA1[s].wait_recv()
        XA2[s] = gsend(chunk(xx(-s), z, cols_a, half_of(s)), xdev(s))
    forward_zb(1)
    start_xb(1)
    start_xb(-1)
    forward_xb(0)
    for s in SIGNS:
        XA2[s].wait_recv()
    for cp in range(2):
        for s in SIGNS:
            ZA[1, s, cp] = gsend(plane(cp, z), zdev(s))
    total = wt[...]
    for d in range(1, NX):
        WX[d - 1].wait_recv()
        total = total + wx[d]
    wz0[...] = total
    WZ = [remote(wz0, wz.at[d], ws.at[d + 2], wr.at[d + 2], zdev(d)) for d in range(1, NZ)]
    fcopy.wait()

    forward_zb(2)
    start_xb(2)
    start_xb(-2)
    forward_xb(1)
    forward_xb(-1)
    finish_xh(0)
    product(0)
    send_half(0)
    ci_root(0)
    forward_zb(3)
    start_xb(3)
    start_xb(-3)
    forward_za(1)
    send_quarters(0)
    finish_xh(1)
    finish_xh(-1)
    product(1)
    send_half(1)
    product(-1)
    send_half(-1)
    ci_root(1)
    ci_root(-1)
    ci_near(0)
    forward_xb(2)
    forward_xb(-2)
    forward_zb(4)
    start_xb(4)
    squares(0)
    send_quarters(1)
    send_quarters(-1)
    forward_za(2)
    finish_xh(2)
    finish_xh(-2)
    product(2)
    send_half(2)
    product(-2)
    send_half(-2)
    ci_root(2)
    ci_root(-2)
    ci_far(0)
    ci_near(1)
    ci_near(-1)
    forward_xb(3)
    forward_xb(-3)
    squares(1)
    squares(-1)
    send_quarters(2)
    send_quarters(-2)
    total = wz0[...]
    for d in range(1, NZ):
        WZ[d - 1].wait_recv()
        total = total + wz[d]
    wz0_all = total
    forward_za(3)
    finish_xh(3)
    finish_xh(-3)
    product(3)
    send_half(3)
    product(-3)
    send_half(-3)
    forward_xb(4)
    ci_root(3)
    ci_root(-3)
    squares(2)
    squares(-2)
    send_quarters(3)
    send_quarters(-3)
    ci_far(1)
    ci_far(-1)
    ci_near(2)
    ci_near(-2)
    forward_za(4)
    finish_xh(4)
    product(4)
    send_half(4)
    ci_root(4)
    squares(3)
    squares(-3)
    send_quarters(4)
    for o in (0, 1, -1):
        ci_last(o)
    squares(4)

    v = V[...]
    lx[0] = v
    LX = [remote(lx.at[0], lx.at[d], ls.at[d - 1], lr.at[d - 1], xdev(d)) for d in range(1, NX)]
    for o in (2, -2):
        ci_far(o)
    for o in (3, -3):
        ci_near(o)
    for cp in LX:
        cp.wait_recv()
    lz0[...] = (lx[0] + lx[1]) + (lx[2] + lx[3])
    LZ = [remote(lz0, lz.at[d], ls.at[d + 2], lr.at[d + 2], zdev(d)) for d in range(1, NZ)]
    ci_near(4)
    for o in (3, -3):
        ci_far(o)
    for o in (2, -2):
        ci_last(o)
    v = lz0[...]
    for d in range(1, NZ):
        LZ[d - 1].wait_recv()
        v = v + lz[d]
    lt0[...] = v
    LT = [
        remote(lt0, lt.at[k], ls.at[k + 9], lr.at[k + 9], fdev(*d)) for k, d in enumerate(fcopies, 1)
    ]
    weights = [wz0_all[0], wz0_all[1]]
    labels = [wz0_all[2], wz0_all[3]]
    ids = lax.broadcasted_iota(jnp.int32, (STRATA, 128), 0).astype(jnp.float32)

    def over_strata(tiles):
        acc = jnp.zeros((STRATA, 128), jnp.float32)
        for cp in range(2):
            for zp in range(NZ):
                acc = acc + jnp.where(labels[cp][zp : zp + 1, :] == ids, tiles[cp][zp : zp + 1, :], 0.0)
        return jnp.sum(acc, axis=1, keepdims=True)

    mass = over_strata(weights)
    ci_far(4)
    for o in (3, -3, 4):
        ci_last(o)
    same, other = lt0[...], None
    for k, (dyk, dck) in enumerate(fcopies, 1):
        LT[k - 1].wait_recv()
        if dck == 0:
            same = same + lt[k]
        else:
            other = lt[k] if other is None else other + lt[k]
    first = c == 0
    raw = [jnp.where(first, same, other), jnp.where(first, other, same)]
    products = [weights[cp] * raw[cp] for cp in range(2)]
    ratio = mass / over_strata(products)
    new_weights = []
    for cp in range(2):
        rows = [
            jnp.sum(jnp.where(labels[cp][zp : zp + 1, :] == ids, ratio, 0.0), axis=0, keepdims=True)
            for zp in range(NZ)
        ]
        row_ratio = jnp.concatenate(rows, axis=0)
        new_weight = products[cp] * row_ratio
        new_weights.append(new_weight)
        step = new_weight - weights[cp]
        for zp in range(NZ):
            cols = pl.ds((cp * NZ + zp) * 128, 128)
            S[:, cols] = (S[:, cols].astype(jnp.float32) * step[zp : zp + 1, :]).astype(jnp.bfloat16)

    def own_rows(tiles):
        tile = jnp.where(x // 2 == 0, tiles[0], tiles[1])
        line = jnp.sum(jnp.where(sub == z, tile, 0.0), axis=0, keepdims=True)
        return jnp.where(x % 2 == 0, line[:, :64], line[:, 64:])

    nw_ref[...] = own_rows(new_weights)
    lev_ref[...] = own_rows(raw) / features

    for cp in pending:
        cp.wait_send()
    for o in OFFSETS:
        ci_finish(o)


def gather(cand, fac, weights, strata):
    rows_dev, feat_block = cand.shape
    row_block = fac.shape[0]
    bf, f32 = jnp.bfloat16, jnp.float32
    vmem = pl.BlockSpec(memory_space=pltpu.VMEM)
    hbm = pl.BlockSpec(memory_space=pltpu.HBM)
    dma = pltpu.SemaphoreType.DMA
    return pl.pallas_call(
        gather_kernel,
        out_shape=(
            pltpu.VMEM((2, NZ, 2, rows_dev, feat_block), bf),
            pltpu.VMEM((row_block, NX * NZ * rows_dev), bf),
            pltpu.VMEM((1, rows_dev), f32),
            pltpu.VMEM((1, rows_dev), f32),
        ),
        in_specs=[hbm, hbm, hbm, hbm],
        out_specs=(vmem, vmem, vmem, vmem),
        scratch_shapes=[
            pltpu.VMEM((1, rows_dev), f32),
            pltpu.VMEM((1, rows_dev), jnp.int32),
            pltpu.VMEM((8, 128), f32),
            pltpu.VMEM((4, NZ, 128), f32),
            pltpu.VMEM(fac.shape, bf),
            pltpu.VMEM((2, NZ, 2, rows_dev, row_block), bf),
            pltpu.VMEM((NZ, 2, row_block, 128), bf),
            pltpu.VMEM((NZ, row_block, 128), bf),
            pltpu.VMEM((NZ, NY, 128, 128), bf),
            pltpu.VMEM((NZ, NY, 128, 128), bf),
            pltpu.VMEM((NZ, 128), f32),
            pltpu.VMEM((NX, 4, NZ, 128), f32),
            pltpu.VMEM((4, NZ, 128), f32),
            pltpu.VMEM((NZ, 4, NZ, 128), f32),
            pltpu.VMEM((NX, NZ, 128), f32),
            pltpu.VMEM((NZ, 128), f32),
            pltpu.VMEM((NZ, NZ, 128), f32),
            pltpu.VMEM((NZ, 128), f32),
            pltpu.VMEM((NZ, NZ, 128), f32),
            dma((4,)),
            dma((58,)),
            dma((58,)),
            dma((10,)),
            dma((10,)),
            dma((8,)),
            dma((8,)),
            dma((24,)),
            dma((24,)),
            dma((24,)),
            dma((8,)),
            dma((17,)),
            dma((17,)),
        ],
        compiler_params=pltpu.CompilerParams(
            collective_id=0, has_side_effects=True, vmem_limit_bytes=40 * 1024 * 1024
        ),
    )(*[
        pltpu.with_memory_space_constraint(a, pltpu.HBM)
        for a in (cand, fac, weights.reshape(1, rows_dev), strata.reshape(1, rows_dev))
    ])


WIDTH = 512


def increment_kernel(s_ref, g_ref, nw_ref, lev_ref, o_hbm, nw_hbm, lev_hbm, out, sem):
    copies = [
        pltpu.make_async_copy(nw_ref, nw_hbm, sem.at[0]),
        pltpu.make_async_copy(lev_ref, lev_hbm, sem.at[1]),
    ]
    for cp in copies:
        cp.start()
    for j in range(out.shape[1] // WIDTH):
        cols = pl.ds(j * WIDTH, WIDTH)
        out[:, cols] = jnp.dot(s_ref[...], g_ref[:, cols], preferred_element_type=jnp.float32)
        cp = pltpu.make_async_copy(out.at[:, cols], o_hbm.at[:, cols], sem.at[2 + j])
        cp.start()
        copies.append(cp)
    for cp in copies:
        cp.wait()


def increment(s, g, nw, lev):
    rows = s.shape[0]
    columns = g.shape[1]
    vmem = pl.BlockSpec(memory_space=pltpu.VMEM)
    hbm = pl.BlockSpec(memory_space=pltpu.HBM)
    f32 = jnp.float32
    return pl.pallas_call(
        increment_kernel,
        out_shape=(pltpu.HBM((rows, columns), f32), pltpu.HBM(nw.shape, f32), pltpu.HBM(lev.shape, f32)),
        in_specs=[vmem] * 4,
        out_specs=(hbm,) * 3,
        scratch_shapes=[
            pltpu.VMEM((rows, columns), f32),
            pltpu.SemaphoreType.DMA((2 + columns // WIDTH,)),
        ],
        compiler_params=pltpu.CompilerParams(vmem_limit_bytes=30 * 1024 * 1024),
    )(s, g, nw, lev)


def per_device(candidates, inv_factor, weights, strata):
    g, s, nw, lev = gather(candidates, inv_factor, weights, strata)
    information, nw, lev = increment(s, g.reshape(-1, g.shape[-1]), nw, lev)
    return (nw.reshape(weights.shape), lev.reshape(weights.shape), information)


def solution(mesh):
    in_specs = (P("row", "feat"), P("row", "feat"), P("row"), P("row"))
    out_specs = (P("row"), P("row"), P("row", "feat"))
    return jax.shard_map(
        per_device, mesh=mesh, in_specs=in_specs, out_specs=out_specs, check_vma=False
    )
```

```python
import functools

import jax
import jax.numpy as jnp
from jax import lax
from jax.experimental import pallas as pl
from jax.experimental.pallas import tpu as pltpu
from jax.sharding import PartitionSpec as P

MESH = pl.DeviceIdType.MESH
NX, NY, NZ, NC = 4, 4, 8, 2
STRATA = 64
CUT = 768
OFFSETS = (0, 1, -1, 2, -2, 3, -3, 4)


def gather_kernel(
    cand, fac, w_hbm, st_hbm,
    G, S, nw_ref, lev_ref,
    w_ref, st_ref, twice, wt, F, Ci, pb, px, ysb, ysr, V, wx, wz0, wz, lz0, lz, lt0, lt,
    loc_sem, gs, gr, ws, wr, pxs, pxr, yss, ysrs, cs, cr, ls, lr,
):
    features = NY * NC * cand.shape[1]
    row, feat = lax.axis_index("row"), lax.axis_index("feat")
    x, z = row // NZ, row % NZ
    y, c = feat // NC, feat % NC

    def xdev(d):
        return (lax.rem(x + d + NX, NX) * NZ + z, feat)

    def zdev(d):
        return (x * NZ + lax.rem(z + d + NZ, NZ), feat)

    def fdev(dy, dc):
        return (row, lax.rem(y + dy, NY) * NC + lax.rem(c + dc, NC))

    plane_peers = sorted(
        ((dx, dz) for dx in range(NX) for dz in range(NZ) if (dx, dz) != (0, 0)),
        key=lambda d: -(min(d[0], NX - d[0]) + min(d[1], NZ - d[1])),
    )
    fcopies = [(dy, dc) for dy in range(NY) for dc in range(NC) if (dy, dc) != (0, 0)]

    def xx(d):
        return lax.rem(x + d + NX, NX)

    def zz(d):
        return lax.rem(z + d + NZ, NZ)

    fcopy = pltpu.make_async_copy(fac, F, loc_sem.at[0])
    smalls = [
        pltpu.make_async_copy(w_hbm, w_ref, loc_sem.at[2]),
        pltpu.make_async_copy(st_hbm, st_ref, loc_sem.at[3]),
    ]
    mine = pltpu.make_async_copy(cand, G.at[x // 2, z, x % 2], loc_sem.at[1])
    mine.start()
    for cp in smalls:
        cp.start()
    fcopy.start()

    barrier = pltpu.get_barrier_semaphore()
    peers = [xdev(1), xdev(-1), zdev(1), zdev(-1), fdev(0, 1)] + [fdev(d, 0) for d in range(1, NY)]
    for dev in peers:
        pl.semaphore_signal(barrier, inc=1, device_id=dev, device_id_type=MESH)
    for cp in smalls:
        cp.wait()
    twice[0:1, 0:64] = w_ref[...]
    twice[0:1, 64:128] = w_ref[...]
    twice[1:2, 0:64] = st_ref[...].astype(jnp.float32)
    twice[1:2, 64:128] = st_ref[...].astype(jnp.float32)
    sub = lax.broadcasted_iota(jnp.int32, (NZ, 128), 0)
    lane = lax.broadcasted_iota(jnp.int32, (NZ, 128), 1)
    here = jnp.logical_and(sub == z, lane // 64 == x % 2)
    for k in range(2):
        placed = jnp.where(here, twice[k : k + 1, :], 0.0)
        for cp in range(2):
            wt[2 * k + cp] = jnp.where(x // 2 == cp, placed, 0.0)

    mine.wait()
    pl.semaphore_wait(barrier, len(peers))

    pending = []

    def remote(src, dst, ssem, rsem, dev, keep=True):
        cp = pltpu.make_async_remote_copy(
            src_ref=src, dst_ref=dst, send_sem=ssem, recv_sem=rsem, device_id=dev, device_id_type=MESH
        )
        cp.start()
        if keep:
            pending.append(cp)
        return cp

    count = [0]

    def gsend(view, dev):
        k = count[0]
        count[0] += 1
        return remote(view, view, gs.at[k], gr.at[k], dev)

    cols_a, cols_b = pl.ds(0, CUT), pl.ds(CUT, cand.shape[1] - CUT)
    rows_dev = cand.shape[0]
    half = rows_dev // 2
    SIGNS = (1, -1)

    def half_of(s):
        return pl.ds(0 if s > 0 else half, half)

    def chunk(xp, zp, cols, rows=None):
        if rows is None:
            rows = pl.ds(0, rows_dev)
        return G.at[xp // 2, zp, xp % 2, rows, cols]

    def plane(cp, zp):
        return G.at[cp, zp, :, :, cols_a]

    XA1, XA2, ZB, ZA, XB, XH = {}, {}, {}, {}, {}, {}

    def start_xb(o):
        for s in SIGNS:
            XB[o, s] = gsend(chunk(x, zz(o), cols_b), xdev(s))

    def forward_xb(o):
        for s in SIGNS:
            XB[o, s].wait_recv()
            XH[o, s] = gsend(chunk(xx(-s), zz(o), cols_b, half_of(s)), xdev(s))

    def finish_xh(o):
        for s in SIGNS:
            XH[o, s].wait_recv()

    def forward_zb(d):
        for s in SIGNS:
            ZB[d, s].wait_recv()
            if d < 3:
                ZB[d + 1, s] = gsend(chunk(x, zz(-s * d), cols_b), zdev(s))
            elif d == 3:
                ZB[d + 1, s] = gsend(chunk(x, zz(-s * d), cols_b, half_of(s)), zdev(s))

    def forward_za(d):
        for cp in range(2):
            for s in SIGNS:
                if (d, s, cp) not in ZA:
                    continue
                ZA[d, s, cp].wait_recv()
                if d < 3 or (d == 3 and cp == (0 if s > 0 else 1)):
                    ZA[d + 1, s, cp] = gsend(plane(cp, zz(-s * d)), zdev(s))

    def product(o):
        zp = zz(o)
        a = G[:, zp].reshape(NX * rows_dev, cand.shape[1])
        for n in range(2):
            rows = pl.ds(n * 256, 256)
            p = lax.dot_general(
                F[rows, :], a, (((1,), (1,)), ((), ())), preferred_element_type=jnp.float32
            ).astype(jnp.bfloat16)
            pb[zp, 0, rows, :] = p[:, :128]
            pb[zp, 1, rows, :] = p[:, 128:]

    PX, YS = {}, {}

    def send_half(o):
        i = OFFSETS.index(o)
        zp = zz(o)
        PX[o] = remote(pb.at[zp, 1 - c], px.at[zp], pxs.at[i], pxr.at[i], fdev(0, 1))

    def send_quarters(o):
        i = OFFSETS.index(o)
        zp = zz(o)
        PX[o].wait_recv()
        q = pb[zp, c].astype(jnp.float32) + px[zp].astype(jnp.float32)
        ysb[zp] = q.astype(jnp.bfloat16).reshape(NY, 128, 128)
        for d in range(1, NY):
            yp = lax.rem(y + d, NY)
            YS[o, d] = remote(
                ysb.at[zp, yp], ysr.at[zp, d], yss.at[i * 3 + d - 1], ysrs.at[i * 3 + d - 1], fdev(d, 0)
            )

    def squares(o):
        zp = zz(o)
        total = ysb[zp, y].astype(jnp.float32)
        for d in range(1, NY):
            YS[o, d].wait_recv()
            total = total + ysr[zp, d].astype(jnp.float32)
        V[pl.ds(zp, 1), :] = jnp.sum(total * total, axis=0, keepdims=True)

    block = Ci.shape[-1]
    col0 = pl.multiple_of((z % 4) * block, block)
    croot = z // 4
    dy = lax.rem(y - x + NY, NY)
    on_core = c == croot
    is_root = jnp.logical_and(dy == 0, on_core)

    def ci_copy(o, slot, src, dev):
        i = OFFSETS.index(o)
        return pltpu.make_async_remote_copy(
            src_ref=src, dst_ref=Ci.at[:, zz(o)], send_sem=cs.at[i * 3 + slot], recv_sem=cr.at[i],
            device_id=dev, device_id_type=MESH,
        )

    def ci_source(o):
        return G.at[:, zz(o), :, :, pl.ds(col0, block)]

    def ci_root(o):
        @pl.when(is_root)
        def _():
            src = ci_source(o)
            ci_copy(o, 0, src, fdev(1, 0)).start()
            ci_copy(o, 1, src, fdev(3, 0)).start()
            ci_copy(o, 2, src, fdev(0, 1)).start()
            own = pltpu.make_async_copy(src, Ci.at[:, zz(o)], cr.at[OFFSETS.index(o)])
            own.start()
            own.wait()

    def ci_wait(o):
        ci_copy(o, 0, Ci.at[:, zz(o)], fdev(0, 1)).wait_recv()

    def ci_near(o):
        i = OFFSETS.index(o)
        for d in (1, 3):
            @pl.when(jnp.logical_and(on_core, dy == d))
            def _():
                ci_wait(o)
                if d == (1 if i % 2 == 0 else 3):
                    ci_copy(o, 0, Ci.at[:, zz(o)], fdev(d, 0)).start()
                ci_copy(o, 2, Ci.at[:, zz(o)], fdev(0, 1)).start()

    def ci_far(o):
        @pl.when(jnp.logical_and(on_core, dy == 2))
        def _():
            ci_wait(o)
            ci_copy(o, 2, Ci.at[:, zz(o)], fdev(0, 1)).start()

    def ci_last(o):
        @pl.when(jnp.logical_not(on_core))
        def _():
            ci_wait(o)

        for cp in range(2):
            t = Ci[cp, zz(o)].reshape(128, block)
            S[:, pl.ds(pl.multiple_of((cp * NZ + zz(o)) * 128, 128), 128)] = t.T

    def ci_finish(o):
        i = OFFSETS.index(o)

        @pl.when(is_root)
        def _():
            for slot in range(3):
                ci_copy(o, slot, ci_source(o), fdev(0, 1)).wait_send()

        for d in (1, 2, 3):
            @pl.when(jnp.logical_and(on_core, dy == d))
            def _():
                if d == (1 if i % 2 == 0 else 3):
                    ci_copy(o, 0, Ci.at[:, zz(o)], fdev(0, 1)).wait_send()
                ci_copy(o, 2, Ci.at[:, zz(o)], fdev(0, 1)).wait_send()

    for s in SIGNS:
        XA1[s] = gsend(chunk(x, z, cols_a), xdev(s))
    for s in SIGNS:
        ZB[1, s] = gsend(chunk(x, z, cols_b), zdev(s))
    start_xb(0)
    for s in SIGNS:
        XA1[s].wait_recv()
        XA2[s] = gsend(chunk(xx(-s), z, cols_a, half_of(s)), xdev(s))
    forward_zb(1)
    start_xb(1)
    start_xb(-1)
    forward_xb(0)
    for s in SIGNS:
        XA2[s].wait_recv()
    for cp in range(2):
        for s in SIGNS:
            ZA[1, s, cp] = gsend(plane(cp, z), zdev(s))
    WX = [remote(wt, wx.at[d], ws.at[d - 1], wr.at[d - 1], xdev(d)) for d in range(1, NX)]
    fcopy.wait()

    forward_zb(2)
    start_xb(2)
    start_xb(-2)
    forward_xb(1)
    forward_xb(-1)
    finish_xh(0)
    ci_root(0)
    product(0)
    send_half(0)
    forward_zb(3)
    start_xb(3)
    start_xb(-3)
    forward_za(1)
    send_quarters(0)
    finish_xh(1)
    finish_xh(-1)
    ci_root(1)
    ci_root(-1)
    product(1)
    send_half(1)
    product(-1)
    send_half(-1)
    ci_near(0)
    forward_xb(2)
    forward_xb(-2)
    forward_zb(4)
    start_xb(4)
    total = wt[...]
    for d in range(1, NX):
        WX[d - 1].wait_recv()
        total = total + wx[d]
    wz0[...] = total
    WZ = [remote(wz0, wz.at[d], ws.at[d + 2], wr.at[d + 2], zdev(d)) for d in range(1, NZ)]
    squares(0)
    send_quarters(1)
    send_quarters(-1)
    forward_za(2)
    finish_xh(2)
    finish_xh(-2)
    ci_root(2)
    ci_root(-2)
    product(2)
    send_half(2)
    product(-2)
    send_half(-2)
    ci_far(0)
    ci_near(1)
    ci_near(-1)
    forward_xb(3)
    forward_xb(-3)
    squares(1)
    squares(-1)
    send_quarters(2)
    send_quarters(-2)
    forward_za(3)
    finish_xh(3)
    finish_xh(-3)
    ci_root(3)
    ci_root(-3)
    product(3)
    send_half(3)
    product(-3)
    send_half(-3)
    forward_xb(4)
    squares(2)
    squares(-2)
    send_quarters(3)
    send_quarters(-3)
    ci_far(1)
    ci_far(-1)
    ci_near(2)
    ci_near(-2)
    forward_za(4)
    total = wz0[...]
    for d in range(1, NZ):
        WZ[d - 1].wait_recv()
        total = total + wz[d]
    wz0_all = total
    finish_xh(4)
    product(4)
    send_half(4)
    send_quarters(4)
    ci_root(4)
    squares(3)
    squares(-3)
    for o in (0, 1, -1):
        ci_last(o)
    squares(4)

    lz0[...] = V[...]
    for k, (dx, dz) in enumerate(plane_peers):
        remote(lz0, lz.at[k], ls.at[0], lr.at[0], (xx(dx) * NZ + zz(dz), feat), keep=False)
    all_sums = pltpu.make_async_remote_copy(
        src_ref=lz, dst_ref=lz, send_sem=ls.at[0], recv_sem=lr.at[0], device_id=xdev(1), device_id_type=MESH
    )
    for o in (2, -2):
        ci_far(o)
    for o in (3, -3):
        ci_near(o)
    ci_near(4)
    for o in (2, -2):
        ci_last(o)
    v = lz0[...]
    all_sums.wait_recv()
    for k in range(len(plane_peers)):
        v = v + lz[k]
    lt0[...] = v
    LT = [
        remote(lt0, lt.at[k], ls.at[k + 9], lr.at[k + 9], fdev(*d)) for k, d in enumerate(fcopies, 1)
    ]
    weights = [wz0_all[0], wz0_all[1]]
    labels = [wz0_all[2], wz0_all[3]]
    ids = lax.broadcasted_iota(jnp.int32, (STRATA, 128), 0).astype(jnp.float32)

    def over_strata(tiles):
        acc = jnp.zeros((STRATA, 128), jnp.float32)
        for cp in range(2):
            for zp in range(NZ):
                acc = acc + jnp.where(labels[cp][zp : zp + 1, :] == ids, tiles[cp][zp : zp + 1, :], 0.0)
        return jnp.sum(acc, axis=1, keepdims=True)

    mass = over_strata(weights)
    all_sums.wait_send()
    for o in (3, -3, 4):
        ci_far(o)
    for o in (3, -3, 4):
        ci_last(o)
    for cp in pending:
        cp.wait_send()
    for o in OFFSETS:
        ci_finish(o)
    same, other = lt0[...], None
    for k, (dyk, dck) in enumerate(fcopies, 1):
        LT[k - 1].wait_recv()
        if dck == 0:
            same = same + lt[k]
        else:
            other = lt[k] if other is None else other + lt[k]
    first = c == 0
    raw = [jnp.where(first, same, other), jnp.where(first, other, same)]
    products = [weights[cp] * raw[cp] for cp in range(2)]
    ratio = mass / over_strata(products)
    new_weights = []
    for cp in range(2):
        rows = [
            jnp.sum(jnp.where(labels[cp][zp : zp + 1, :] == ids, ratio, 0.0), axis=0, keepdims=True)
            for zp in range(NZ)
        ]
        row_ratio = jnp.concatenate(rows, axis=0)
        new_weight = products[cp] * row_ratio
        new_weights.append(new_weight)
        step = new_weight - weights[cp]
        for zp in range(NZ):
            cols = pl.ds((cp * NZ + zp) * 128, 128)
            S[:, cols] = (S[:, cols].astype(jnp.float32) * step[zp : zp + 1, :]).astype(jnp.bfloat16)

    def own_rows(tiles):
        tile = jnp.where(x // 2 == 0, tiles[0], tiles[1])
        line = jnp.sum(jnp.where(sub == z, tile, 0.0), axis=0, keepdims=True)
        return jnp.where(x % 2 == 0, line[:, :64], line[:, 64:])

    nw_ref[...] = own_rows(new_weights)
    lev_ref[...] = own_rows(raw) / features


def gather(cand, fac, weights, strata):
    rows_dev, feat_block = cand.shape
    row_block = fac.shape[0]
    bf, f32 = jnp.bfloat16, jnp.float32
    vmem = pl.BlockSpec(memory_space=pltpu.VMEM)
    hbm = pl.BlockSpec(memory_space=pltpu.HBM)
    dma = pltpu.SemaphoreType.DMA
    return pl.pallas_call(
        gather_kernel,
        out_shape=(
            pltpu.VMEM((2, NZ, 2, rows_dev, feat_block), bf),
            pltpu.VMEM((row_block, NX * NZ * rows_dev), bf),
            pltpu.VMEM((1, rows_dev), f32),
            pltpu.VMEM((1, rows_dev), f32),
        ),
        in_specs=[hbm, hbm, hbm, hbm],
        out_specs=(vmem, vmem, vmem, vmem),
        scratch_shapes=[
            pltpu.VMEM((1, rows_dev), f32),
            pltpu.VMEM((1, rows_dev), jnp.int32),
            pltpu.VMEM((8, 128), f32),
            pltpu.VMEM((4, NZ, 128), f32),
            pltpu.VMEM(fac.shape, bf),
            pltpu.VMEM((2, NZ, 2, rows_dev, row_block), bf),
            pltpu.VMEM((NZ, 2, row_block, 128), bf),
            pltpu.VMEM((NZ, row_block, 128), bf),
            pltpu.VMEM((NZ, NY, 128, 128), bf),
            pltpu.VMEM((NZ, NY, 128, 128), bf),
            pltpu.VMEM((NZ, 128), f32),
            pltpu.VMEM((NX, 4, NZ, 128), f32),
            pltpu.VMEM((4, NZ, 128), f32),
            pltpu.VMEM((NZ, 4, NZ, 128), f32),
            pltpu.VMEM((NZ, 128), f32),
            pltpu.VMEM((NX * NZ - 1, NZ, 128), f32),
            pltpu.VMEM((NZ, 128), f32),
            pltpu.VMEM((NZ, NZ, 128), f32),
            dma((4,)),
            dma((58,)),
            dma((58,)),
            dma((10,)),
            dma((10,)),
            dma((8,)),
            dma((8,)),
            dma((24,)),
            dma((24,)),
            dma((24,)),
            dma((8,)),
            dma((17,)),
            dma((17,)),
        ],
        compiler_params=pltpu.CompilerParams(
            collective_id=0, has_side_effects=True, vmem_limit_bytes=40 * 1024 * 1024
        ),
    )(*[
        pltpu.with_memory_space_constraint(a, pltpu.HBM)
        for a in (cand, fac, weights.reshape(1, rows_dev), strata.reshape(1, rows_dev))
    ])


WIDTH = 512


def increment_kernel(s_ref, g_ref, nw_ref, lev_ref, o_hbm, nw_hbm, lev_hbm, out, sem):
    copies = [
        pltpu.make_async_copy(nw_ref, nw_hbm, sem.at[0]),
        pltpu.make_async_copy(lev_ref, lev_hbm, sem.at[1]),
    ]
    for cp in copies:
        cp.start()
    for j in range(out.shape[1] // WIDTH):
        cols = pl.ds(j * WIDTH, WIDTH)
        out[:, cols] = jnp.dot(s_ref[...], g_ref[:, cols], preferred_element_type=jnp.float32)
        cp = pltpu.make_async_copy(out.at[:, cols], o_hbm.at[:, cols], sem.at[2 + j])
        cp.start()
        copies.append(cp)
    for cp in copies:
        cp.wait()


def increment(s, g, nw, lev):
    rows = s.shape[0]
    columns = g.shape[1]
    vmem = pl.BlockSpec(memory_space=pltpu.VMEM)
    hbm = pl.BlockSpec(memory_space=pltpu.HBM)
    f32 = jnp.float32
    return pl.pallas_call(
        increment_kernel,
        out_shape=(pltpu.HBM((rows, columns), f32), pltpu.HBM(nw.shape, f32), pltpu.HBM(lev.shape, f32)),
        in_specs=[vmem] * 4,
        out_specs=(hbm,) * 3,
        scratch_shapes=[
            pltpu.VMEM((rows, columns), f32),
            pltpu.SemaphoreType.DMA((2 + columns // WIDTH,)),
        ],
        compiler_params=pltpu.CompilerParams(vmem_limit_bytes=30 * 1024 * 1024),
    )(s, g, nw, lev)


def per_device(candidates, inv_factor, weights, strata):
    g, s, nw, lev = gather(candidates, inv_factor, weights, strata)
    information, nw, lev = increment(s, g.reshape(-1, g.shape[-1]), nw, lev)
    return (nw.reshape(weights.shape), lev.reshape(weights.shape), information)


def solution(mesh):
    in_specs = (P("row", "feat"), P("row", "feat"), P("row"), P("row"))
    out_specs = (P("row"), P("row"), P("row", "feat"))
    return jax.shard_map(
        per_device, mesh=mesh, in_specs=in_specs, out_specs=out_specs, check_vma=False
    )
```

```python
import functools

import jax
import jax.numpy as jnp
from jax import lax
from jax.experimental import pallas as pl
from jax.experimental.pallas import tpu as pltpu
from jax.sharding import PartitionSpec as P

MESH = pl.DeviceIdType.MESH
NX, NY, NZ, NC = 4, 4, 8, 2
STRATA = 64
OFFSETS = (0, 1, -1, 2, -2, 3, -3, 4)
CUT_OWN, CUT_NEXT, CUT_FAR = 896, 768, 896
XA1, XA2, ZB, XB, XH, ZA, PRODUCT, QUARTERS, SQUARES, NEAR, FAR = range(11)
ORDER = (
    (ZB, 1, -1), (ZB, 1, 1), (XA1, -1), (XA1, 1), (XB, 0, -1), (XB, 0, 1), (ZA, 1, -1, 0), (ZA, 1, 1, 0),
    (XA2, -1), (ZA, 1, -1, 1), (XA2, 1), (ZA, 1, 1, 1), (ZA, 1, -1, -1), (ZA, 1, 1, -1), (XB, 1, -1),
    (XB, 1, 1), (ZB, 2, -1), (ZB, 2, 1), (XB, -1, -1), (XB, -1, 1), (ZA, 1, -1, 2), (ZA, 1, 1, 2),
    (XH, 0, -1), (XH, 0, 1), (ZA, 2, -1, 0), (ZA, 2, 1, 0), (XH, 1, -1), (XH, 1, 1), (ZA, 2, -1, 1),
    (ZA, 2, 1, 1), (XB, 2, -1), (XB, 2, 1), (ZB, 3, -1), (ZB, 3, 1), (XH, -1, -1), (XH, -1, 1), (PRODUCT, 0),
    (XB, -2, -1), (XB, -2, 1), (PRODUCT, 1), (ZA, 2, -1, -1), (ZA, 2, 1, -1), (QUARTERS, 0), (QUARTERS, 1),
    (ZA, 2, -1, 2), (ZA, 2, 1, 2), (XH, 2, -1), (XH, 2, 1), (SQUARES, 0), (PRODUCT, -1), (ZA, 3, -1, 0),
    (ZA, 3, 1, 0), (SQUARES, 1), (XB, 3, -1), (XB, 3, 1), (QUARTERS, -1), (NEAR, 0), (ZB, 4, -1), (ZB, 4, 1),
    (XB, -3, -1), (XB, -3, 1), (NEAR, 1), (ZA, 3, -1, 1), (ZA, 3, 1, 1), (SQUARES, -1), (PRODUCT, 2),
    (ZA, 3, -1, -1), (ZA, 3, 1, -1), (XH, -2, -1), (XH, -2, 1), (QUARTERS, 2), (ZA, 3, -1, 2), (ZA, 3, 1, 2),
    (NEAR, -1), (XH, 3, -1), (XH, 3, 1), (XB, 4, -1), (XB, 4, 1), (ZA, 4, 1, 0), (SQUARES, 2), (FAR, 0),
    (ZA, 4, 1, 1), (FAR, 1), (XH, -3, -1), (XH, -3, 1), (PRODUCT, -2), (ZA, 4, -1, -1), (NEAR, 2),
    (QUARTERS, -2), (ZA, 4, -1, 2), (PRODUCT, 3), (FAR, -1), (QUARTERS, 3), (XH, 4, -1), (XH, 4, 1),
    (SQUARES, -2), (PRODUCT, -3), (SQUARES, 3), (QUARTERS, -3), (PRODUCT, 4), (QUARTERS, 4), (SQUARES, -3),
    (SQUARES, 4),
)


def gather_kernel(
    cand, fac, w_hbm, st_hbm,
    G, S, nw_ref, lev_ref,
    w_ref, st_ref, twice, wt, F, Ci, pb, px, ysb, ysr, V, wx, wz0, wz, lz0, lz, lt0, lt,
    loc_sem, gs, gr, ws, wr, pxs, pxr, yss, ysrs, cs, cr, ls, lr,
):
    features = NY * NC * cand.shape[1]
    row, feat = lax.axis_index("row"), lax.axis_index("feat")
    x, z = row // NZ, row % NZ
    y, c = feat // NC, feat % NC

    def xdev(d):
        return (lax.rem(x + d + NX, NX) * NZ + z, feat)

    def zdev(d):
        return (x * NZ + lax.rem(z + d + NZ, NZ), feat)

    def fdev(dy, dc):
        return (row, lax.rem(y + dy, NY) * NC + lax.rem(c + dc, NC))

    plane_peers = sorted(
        ((dx, dz) for dx in range(NX) for dz in range(NZ) if (dx, dz) != (0, 0)),
        key=lambda d: -(min(d[0], NX - d[0]) + min(d[1], NZ - d[1])),
    )
    fcopies = [(dy, dc) for dy in range(NY) for dc in range(NC) if (dy, dc) != (0, 0)]

    def xx(d):
        return lax.rem(x + d + NX, NX)

    def zz(d):
        return lax.rem(z + d + NZ, NZ)

    fcopy = pltpu.make_async_copy(fac, F, loc_sem.at[0])
    smalls = [
        pltpu.make_async_copy(w_hbm, w_ref, loc_sem.at[2]),
        pltpu.make_async_copy(st_hbm, st_ref, loc_sem.at[3]),
    ]
    mine = pltpu.make_async_copy(cand, G.at[x // 2, z, x % 2], loc_sem.at[1])
    mine.start()
    for cp in smalls:
        cp.start()
    fcopy.start()

    barrier = pltpu.get_barrier_semaphore()
    peers = [xdev(1), xdev(-1), zdev(1), zdev(-1), fdev(0, 1)] + [fdev(d, 0) for d in range(1, NY)]
    for dev in peers:
        pl.semaphore_signal(barrier, inc=1, device_id=dev, device_id_type=MESH)
    for cp in smalls:
        cp.wait()
    twice[0:1, 0:64] = w_ref[...]
    twice[0:1, 64:128] = w_ref[...]
    twice[1:2, 0:64] = st_ref[...].astype(jnp.float32)
    twice[1:2, 64:128] = st_ref[...].astype(jnp.float32)
    sub = lax.broadcasted_iota(jnp.int32, (NZ, 128), 0)
    lane = lax.broadcasted_iota(jnp.int32, (NZ, 128), 1)
    here = jnp.logical_and(sub == z, lane // 64 == x % 2)
    for k in range(2):
        placed = jnp.where(here, twice[k : k + 1, :], 0.0)
        for cp in range(2):
            wt[2 * k + cp] = jnp.where(x // 2 == cp, placed, 0.0)

    mine.wait()
    pl.semaphore_wait(barrier, len(peers))

    pending = []

    def remote(src, dst, ssem, rsem, dev, keep=True):
        cp = pltpu.make_async_remote_copy(
            src_ref=src, dst_ref=dst, send_sem=ssem, recv_sem=rsem, device_id=dev, device_id_type=MESH
        )
        cp.start()
        if keep:
            pending.append(cp)
        return cp

    count = [0]

    def gsend(view, dev):
        k = count[0]
        count[0] += 1
        return remote(view, view, gs.at[k], gr.at[k], dev)

    columns = cand.shape[1]
    rows_dev = cand.shape[0]
    half = rows_dev // 2

    def chunk(dx, dz, first, last, side=0):
        xp, zp = xx(dx), zz(dz)
        rows = {0: pl.ds(0, rows_dev), 1: pl.ds(0, half), -1: pl.ds(half, half)}[side]
        return G.at[xp // 2, zp, xp % 2, rows, pl.ds(first, last - first)]

    def own_column(o):
        if o == 0:
            return []
        return [(ZB, 4, 1), (ZB, 4, -1)] if o == 4 else [(ZB, abs(o), -1 if o > 0 else 1)]

    def message(kind, *at):
        if kind == XA1:
            (s,) = at
            return chunk(0, 0, 0, CUT_OWN), xdev(s), []
        if kind == XA2:
            (s,) = at
            return chunk(-s, 0, 0, CUT_OWN, s), xdev(s), [(XA1, s)]
        if kind == ZB:
            d, s = at
            side = s if d == 4 else 0
            return chunk(0, -s * (d - 1), CUT_NEXT, columns, side), zdev(s), [(ZB, d - 1, s)] if d > 1 else []
        if kind == XB:
            o, s = at
            return chunk(0, o, CUT_NEXT if o else CUT_OWN, columns), xdev(s), own_column(o)
        if kind == XH:
            o, s = at
            return chunk(-s, o, CUT_FAR if o else CUT_OWN, columns, s), xdev(s), [(XB, o, s)]
        d, s, r = at
        first = {0: [], 1: [(XA1, -1)], -1: [(XA1, 1)], 2: [(XA2, 1), (XA2, -1)]}[r]
        after = [(ZA, d - 1, s, r)] if d > 1 else first
        return chunk(r, -s * (d - 1), 0, CUT_FAR if r == 2 else CUT_NEXT), zdev(s), after

    def whole(o):
        keys = [(kind, o, s) for kind in (XB, XH) for s in (1, -1)] + own_column(o)
        if o == 0:
            return keys + [(kind, s) for kind in (XA1, XA2) for s in (1, -1)]
        if o == 4:
            return keys + [(ZA, 4, 1, 0), (ZA, 4, 1, 1), (ZA, 4, -1, 2), (ZA, 4, -1, -1)]
        return keys + [(ZA, abs(o), -1 if o > 0 else 1, r) for r in (0, 1, -1, 2)]

    sent, received = {}, set()

    def receive(keys):
        for key in keys:
            if key not in received:
                received.add(key)
                sent[key].wait_recv()

    def product(o):
        zp = zz(o)
        a = G[:, zp].reshape(NX * rows_dev, cand.shape[1])
        for n in range(2):
            rows = pl.ds(n * 256, 256)
            p = lax.dot_general(
                F[rows, :], a, (((1,), (1,)), ((), ())), preferred_element_type=jnp.float32
            ).astype(jnp.bfloat16)
            pb[zp, 0, rows, :] = p[:, :128]
            pb[zp, 1, rows, :] = p[:, 128:]

    PX, YS = {}, {}

    def send_half(o):
        i = OFFSETS.index(o)
        zp = zz(o)
        PX[o] = remote(pb.at[zp, 1 - c], px.at[zp], pxs.at[i], pxr.at[i], fdev(0, 1))

    def send_quarters(o):
        i = OFFSETS.index(o)
        zp = zz(o)
        PX[o].wait_recv()
        q = pb[zp, c].astype(jnp.float32) + px[zp].astype(jnp.float32)
        ysb[zp] = q.astype(jnp.bfloat16).reshape(NY, 128, 128)
        for d in range(1, NY):
            yp = lax.rem(y + d, NY)
            YS[o, d] = remote(
                ysb.at[zp, yp], ysr.at[zp, d], yss.at[i * 3 + d - 1], ysrs.at[i * 3 + d - 1], fdev(d, 0)
            )

    def squares(o):
        zp = zz(o)
        total = ysb[zp, y].astype(jnp.float32)
        for d in range(1, NY):
            YS[o, d].wait_recv()
            total = total + ysr[zp, d].astype(jnp.float32)
        V[pl.ds(zp, 1), :] = jnp.sum(total * total, axis=0, keepdims=True)

    block = Ci.shape[-1]
    col0 = pl.multiple_of((z % 4) * block, block)
    croot = z // 4
    dy = lax.rem(y - x + NY, NY)
    on_core = c == croot
    is_root = jnp.logical_and(dy == 0, on_core)

    def ci_copy(o, slot, src, dev):
        i = OFFSETS.index(o)
        return pltpu.make_async_remote_copy(
            src_ref=src, dst_ref=Ci.at[:, zz(o)], send_sem=cs.at[i * 3 + slot], recv_sem=cr.at[i],
            device_id=dev, device_id_type=MESH,
        )

    def ci_source(o):
        return G.at[:, zz(o), :, :, pl.ds(col0, block)]

    def ci_root(o):
        @pl.when(is_root)
        def _():
            src = ci_source(o)
            ci_copy(o, 0, src, fdev(1, 0)).start()
            ci_copy(o, 1, src, fdev(3, 0)).start()
            ci_copy(o, 2, src, fdev(0, 1)).start()
            own = pltpu.make_async_copy(src, Ci.at[:, zz(o)], cr.at[OFFSETS.index(o)])
            own.start()
            own.wait()

    def ci_wait(o):
        ci_copy(o, 0, Ci.at[:, zz(o)], fdev(0, 1)).wait_recv()

    def ci_near(o):
        i = OFFSETS.index(o)
        for d in (1, 3):
            @pl.when(jnp.logical_and(on_core, dy == d))
            def _():
                ci_wait(o)
                if d == (1 if i % 2 == 0 else 3):
                    ci_copy(o, 0, Ci.at[:, zz(o)], fdev(d, 0)).start()
                ci_copy(o, 2, Ci.at[:, zz(o)], fdev(0, 1)).start()

    def ci_far(o):
        @pl.when(jnp.logical_and(on_core, dy == 2))
        def _():
            ci_wait(o)
            ci_copy(o, 2, Ci.at[:, zz(o)], fdev(0, 1)).start()

    def ci_last(o):
        @pl.when(jnp.logical_not(on_core))
        def _():
            ci_wait(o)

        for cp in range(2):
            t = Ci[cp, zz(o)].reshape(128, block)
            S[:, pl.ds(pl.multiple_of((cp * NZ + zz(o)) * 128, 128), 128)] = t.T

    def ci_finish(o):
        i = OFFSETS.index(o)

        @pl.when(is_root)
        def _():
            for slot in range(3):
                ci_copy(o, slot, ci_source(o), fdev(0, 1)).wait_send()

        for d in (1, 2, 3):
            @pl.when(jnp.logical_and(on_core, dy == d))
            def _():
                if d == (1 if i % 2 == 0 else 3):
                    ci_copy(o, 0, Ci.at[:, zz(o)], fdev(0, 1)).wait_send()
                ci_copy(o, 2, Ci.at[:, zz(o)], fdev(0, 1)).wait_send()

    WX, WZ = [], []
    near, far = [], []
    for op in ORDER:
        kind, at = op[0], op[1:]
        if kind <= ZA:
            view, dev, after = message(*op)
            receive(after)
            sent[op] = gsend(view, dev)
        elif kind == PRODUCT:
            (o,) = at
            receive(whole(o))
            if o == 0:
                fcopy.wait()
            if o != 4:
                ci_root(o)
            product(o)
            send_half(o)
            if o == 0:
                WX = [remote(wt, wx.at[d], ws.at[d - 1], wr.at[d - 1], xdev(d)) for d in range(1, NX)]
            if o == -2:
                total = wt[...]
                for d in range(1, NX):
                    WX[d - 1].wait_recv()
                    total = total + wx[d]
                wz0[...] = total
                receive(own_column(4))
                WZ = [remote(wz0, wz.at[d], ws.at[d + 2], wr.at[d + 2], zdev(d)) for d in range(1, NZ)]
        elif kind == QUARTERS:
            send_quarters(*at)
            if at == (4,):
                ci_root(4)
                for o in OFFSETS[:-1]:
                    if o not in near:
                        ci_near(o)
                        near.append(o)
                last = list(far)
                for o in last:
                    ci_last(o)
        elif kind == SQUARES:
            squares(*at)
        elif kind == NEAR:
            ci_near(*at)
            near += at
        else:
            ci_far(*at)
            far += at

    lz0[...] = V[...]
    for k, (dx, dz) in enumerate(plane_peers):
        remote(lz0, lz.at[k], ls.at[0], lr.at[0], (xx(dx) * NZ + zz(dz), feat), keep=False)
    all_sums = pltpu.make_async_remote_copy(
        src_ref=lz, dst_ref=lz, send_sem=ls.at[0], recv_sem=lr.at[0], device_id=xdev(1), device_id_type=MESH
    )
    ci_near(4)
    for o in OFFSETS[:-1]:
        if o not in far:
            ci_far(o)
            far.append(o)
    total = wz0[...]
    for d in range(1, NZ):
        WZ[d - 1].wait_recv()
        total = total + wz[d]
    wz0_all = total
    v = lz0[...]
    all_sums.wait_recv()
    for k in range(len(plane_peers)):
        v = v + lz[k]
    lt0[...] = v
    LT = [
        remote(lt0, lt.at[k], ls.at[k + 9], lr.at[k + 9], fdev(*d)) for k, d in enumerate(fcopies, 1)
    ]
    weights = [wz0_all[0], wz0_all[1]]
    labels = [wz0_all[2], wz0_all[3]]
    ids = lax.broadcasted_iota(jnp.int32, (STRATA, 128), 0).astype(jnp.float32)

    def over_strata(tiles):
        acc = jnp.zeros((STRATA, 128), jnp.float32)
        for cp in range(2):
            for zp in range(NZ):
                acc = acc + jnp.where(labels[cp][zp : zp + 1, :] == ids, tiles[cp][zp : zp + 1, :], 0.0)
        return jnp.sum(acc, axis=1, keepdims=True)

    mass = over_strata(weights)
    all_sums.wait_send()
    for o in OFFSETS:
        if o not in far:
            ci_far(o)
    for o in OFFSETS:
        if o not in last:
            ci_last(o)
    for cp in pending:
        cp.wait_send()
    for o in OFFSETS:
        ci_finish(o)
    same, other = lt0[...], None
    for k, (dyk, dck) in enumerate(fcopies, 1):
        LT[k - 1].wait_recv()
        if dck == 0:
            same = same + lt[k]
        else:
            other = lt[k] if other is None else other + lt[k]
    first = c == 0
    raw = [jnp.where(first, same, other), jnp.where(first, other, same)]
    products = [weights[cp] * raw[cp] for cp in range(2)]
    ratio = mass / over_strata(products)
    new_weights = []
    for cp in range(2):
        rows = [
            jnp.sum(jnp.where(labels[cp][zp : zp + 1, :] == ids, ratio, 0.0), axis=0, keepdims=True)
            for zp in range(NZ)
        ]
        row_ratio = jnp.concatenate(rows, axis=0)
        new_weight = products[cp] * row_ratio
        new_weights.append(new_weight)
        step = new_weight - weights[cp]
        for zp in range(NZ):
            cols = pl.ds((cp * NZ + zp) * 128, 128)
            S[:, cols] = (S[:, cols].astype(jnp.float32) * step[zp : zp + 1, :]).astype(jnp.bfloat16)

    def own_rows(tiles):
        tile = jnp.where(x // 2 == 0, tiles[0], tiles[1])
        line = jnp.sum(jnp.where(sub == z, tile, 0.0), axis=0, keepdims=True)
        return jnp.where(x % 2 == 0, line[:, :64], line[:, 64:])

    nw_ref[...] = own_rows(new_weights)
    lev_ref[...] = own_rows(raw) / features


def gather(cand, fac, weights, strata):
    rows_dev, feat_block = cand.shape
    row_block = fac.shape[0]
    bf, f32 = jnp.bfloat16, jnp.float32
    vmem = pl.BlockSpec(memory_space=pltpu.VMEM)
    hbm = pl.BlockSpec(memory_space=pltpu.HBM)
    dma = pltpu.SemaphoreType.DMA
    return pl.pallas_call(
        gather_kernel,
        out_shape=(
            pltpu.VMEM((2, NZ, 2, rows_dev, feat_block), bf),
            pltpu.VMEM((row_block, NX * NZ * rows_dev), bf),
            pltpu.VMEM((1, rows_dev), f32),
            pltpu.VMEM((1, rows_dev), f32),
        ),
        in_specs=[hbm, hbm, hbm, hbm],
        out_specs=(vmem, vmem, vmem, vmem),
        scratch_shapes=[
            pltpu.VMEM((1, rows_dev), f32),
            pltpu.VMEM((1, rows_dev), jnp.int32),
            pltpu.VMEM((8, 128), f32),
            pltpu.VMEM((4, NZ, 128), f32),
            pltpu.VMEM(fac.shape, bf),
            pltpu.VMEM((2, NZ, 2, rows_dev, row_block), bf),
            pltpu.VMEM((NZ, 2, row_block, 128), bf),
            pltpu.VMEM((NZ, row_block, 128), bf),
            pltpu.VMEM((NZ, NY, 128, 128), bf),
            pltpu.VMEM((NZ, NY, 128, 128), bf),
            pltpu.VMEM((NZ, 128), f32),
            pltpu.VMEM((NX, 4, NZ, 128), f32),
            pltpu.VMEM((4, NZ, 128), f32),
            pltpu.VMEM((NZ, 4, NZ, 128), f32),
            pltpu.VMEM((NZ, 128), f32),
            pltpu.VMEM((NX * NZ - 1, NZ, 128), f32),
            pltpu.VMEM((NZ, 128), f32),
            pltpu.VMEM((NZ, NZ, 128), f32),
            dma((4,)),
            dma((72,)),
            dma((72,)),
            dma((10,)),
            dma((10,)),
            dma((8,)),
            dma((8,)),
            dma((24,)),
            dma((24,)),
            dma((24,)),
            dma((8,)),
            dma((17,)),
            dma((17,)),
        ],
        compiler_params=pltpu.CompilerParams(
            collective_id=0, has_side_effects=True, vmem_limit_bytes=40 * 1024 * 1024
        ),
    )(*[
        pltpu.with_memory_space_constraint(a, pltpu.HBM)
        for a in (cand, fac, weights.reshape(1, rows_dev), strata.reshape(1, rows_dev))
    ])


WIDTH = 512


def increment_kernel(s_ref, g_ref, nw_ref, lev_ref, o_hbm, nw_hbm, lev_hbm, out, sem):
    copies = [
        pltpu.make_async_copy(nw_ref, nw_hbm, sem.at[0]),
        pltpu.make_async_copy(lev_ref, lev_hbm, sem.at[1]),
    ]
    for cp in copies:
        cp.start()
    for j in range(out.shape[1] // WIDTH):
        cols = pl.ds(j * WIDTH, WIDTH)
        out[:, cols] = jnp.dot(s_ref[...], g_ref[:, cols], preferred_element_type=jnp.float32)
        cp = pltpu.make_async_copy(out.at[:, cols], o_hbm.at[:, cols], sem.at[2 + j])
        cp.start()
        copies.append(cp)
    for cp in copies:
        cp.wait()


def increment(s, g, nw, lev):
    rows = s.shape[0]
    columns = g.shape[1]
    vmem = pl.BlockSpec(memory_space=pltpu.VMEM)
    hbm = pl.BlockSpec(memory_space=pltpu.HBM)
    f32 = jnp.float32
    return pl.pallas_call(
        increment_kernel,
        out_shape=(pltpu.HBM((rows, columns), f32), pltpu.HBM(nw.shape, f32), pltpu.HBM(lev.shape, f32)),
        in_specs=[vmem] * 4,
        out_specs=(hbm,) * 3,
        scratch_shapes=[
            pltpu.VMEM((rows, columns), f32),
            pltpu.SemaphoreType.DMA((2 + columns // WIDTH,)),
        ],
        compiler_params=pltpu.CompilerParams(vmem_limit_bytes=30 * 1024 * 1024),
    )(s, g, nw, lev)


def per_device(candidates, inv_factor, weights, strata):
    g, s, nw, lev = gather(candidates, inv_factor, weights, strata)
    information, nw, lev = increment(s, g.reshape(-1, g.shape[-1]), nw, lev)
    return (nw.reshape(weights.shape), lev.reshape(weights.shape), information)


def solution(mesh):
    in_specs = (P("row", "feat"), P("row", "feat"), P("row"), P("row"))
    out_specs = (P("row"), P("row"), P("row", "feat"))
    return jax.shard_map(
        per_device, mesh=mesh, in_specs=in_specs, out_specs=out_specs, check_vma=False
    )
```

```python
import functools

import jax
import jax.numpy as jnp
from jax import lax
from jax.experimental import pallas as pl
from jax.experimental.pallas import tpu as pltpu
from jax.sharding import PartitionSpec as P

MESH = pl.DeviceIdType.MESH
NX, NY, NZ, NC = 4, 4, 8, 2
STRATA = 64
OFFSETS = (0, 1, -1, 2, -2, 3, -3, 4)
CUT_OWN, CUT_NEXT, CUT_FAR = 896, 768, 896
XA1, XA2, ZB, XB, XH, ZA, PRODUCT, QUARTERS, SQUARES, NEAR, FAR = range(11)
ORDER = (
    (ZB, 1, -1), (ZB, 1, 1), (XA1, -1), (XA1, 1), (XB, 0, -1), (XB, 0, 1), (ZA, 1, -1, 0), (ZA, 1, 1, 0),
    (XA2, -1), (ZA, 1, -1, 1), (XA2, 1), (ZA, 1, 1, 1), (XB, 1, -1), (XB, 1, 1), (ZB, 2, -1), (ZB, 2, 1),
    (XH, 0, -1), (XH, 0, 1), (ZA, 1, -1, -1), (ZA, 1, 1, -1), (XB, -1, -1), (XB, -1, 1), (ZA, 1, -1, 2),
    (ZA, 1, 1, 2), (XH, 1, -1), (XH, 1, 1), (ZB, 3, -1), (ZB, 3, 1), (PRODUCT, 0), (XB, 2, -1), (XB, 2, 1),
    (QUARTERS, 0), (ZA, 2, -1, 0), (ZA, 2, 1, 0), (XH, -1, -1), (XH, -1, 1), (PRODUCT, 1), (ZA, 2, -1, 1),
    (ZA, 2, 1, 1), (XB, -2, -1), (XB, -2, 1), (SQUARES, 0), (QUARTERS, 1), (ZB, 4, -1), (ZB, 4, 1), (NEAR, 0),
    (ZA, 2, -1, -1), (ZA, 2, 1, -1), (XH, 2, -1), (XH, 2, 1), (PRODUCT, -1), (ZA, 2, -1, 2), (ZA, 2, 1, 2),
    (XB, 3, -1), (XB, 3, 1), (SQUARES, 1), (QUARTERS, -1), (NEAR, 1), (ZA, 3, -1, 0), (ZA, 3, 1, 0),
    (XH, -2, -1), (XH, -2, 1), (SQUARES, -1), (ZA, 3, -1, 1), (ZA, 3, 1, 1), (XB, -3, -1), (XB, -3, 1),
    (PRODUCT, 2), (ZA, 3, -1, -1), (ZA, 3, 1, -1), (FAR, 0), (NEAR, -1), (QUARTERS, 2), (XH, 3, -1),
    (XH, 3, 1), (ZA, 3, -1, 2), (ZA, 3, 1, 2), (PRODUCT, -2), (XB, 4, -1), (XB, 4, 1), (QUARTERS, -2),
    (ZA, 4, 1, 0), (FAR, 1), (SQUARES, 2), (ZA, 4, -1, -1), (ZA, 4, 1, 1), (XH, -3, -1), (XH, -3, 1),
    (SQUARES, -2), (NEAR, 2), (ZA, 4, -1, 2), (PRODUCT, 3), (QUARTERS, 3), (FAR, -1), (NEAR, -2), (XH, 4, -1),
    (XH, 4, 1), (PRODUCT, -3), (SQUARES, 3), (QUARTERS, -3), (PRODUCT, 4), (QUARTERS, 4), (SQUARES, -3),
    (SQUARES, 4),
)


def gather_kernel(
    cand, fac, w_hbm, st_hbm,
    G, S, nw_ref, lev_ref,
    w_ref, st_ref, twice, wt, F, Ci, pb, px, ysb, ysr, V, wx, wz0, wz, lz0, lz, lt0, lt,
    loc_sem, gs, gr, ws, wr, pxs, pxr, yss, ysrs, cs, cr, ls, lr,
):
    features = NY * NC * cand.shape[1]
    row, feat = lax.axis_index("row"), lax.axis_index("feat")
    x, z = row // NZ, row % NZ
    y, c = feat // NC, feat % NC

    def xdev(d):
        return (lax.rem(x + d + NX, NX) * NZ + z, feat)

    def zdev(d):
        return (x * NZ + lax.rem(z + d + NZ, NZ), feat)

    def fdev(dy, dc):
        return (row, lax.rem(y + dy, NY) * NC + lax.rem(c + dc, NC))

    plane_peers = sorted(
        ((dx, dz) for dx in range(NX) for dz in range(NZ) if (dx, dz) != (0, 0)),
        key=lambda d: -(min(d[0], NX - d[0]) + min(d[1], NZ - d[1])),
    )
    fcopies = [(dy, dc) for dy in (2, 1, 3, 0) for dc in range(NC) if (dy, dc) != (0, 0)]

    def xx(d):
        return lax.rem(x + d + NX, NX)

    def zz(d):
        return lax.rem(z + d + NZ, NZ)

    fcopy = pltpu.make_async_copy(fac, F, loc_sem.at[0])
    smalls = [
        pltpu.make_async_copy(w_hbm, w_ref, loc_sem.at[2]),
        pltpu.make_async_copy(st_hbm, st_ref, loc_sem.at[3]),
    ]
    mine = pltpu.make_async_copy(cand, G.at[x // 2, z, x % 2], loc_sem.at[1])
    mine.start()
    for cp in smalls:
        cp.start()
    fcopy.start()

    barrier = pltpu.get_barrier_semaphore()
    peers = [xdev(1), xdev(-1), zdev(1), zdev(-1), fdev(0, 1)] + [fdev(d, 0) for d in range(1, NY)]
    for dev in peers:
        pl.semaphore_signal(barrier, inc=1, device_id=dev, device_id_type=MESH)
    for cp in smalls:
        cp.wait()
    twice[0:1, 0:64] = w_ref[...]
    twice[0:1, 64:128] = w_ref[...]
    twice[1:2, 0:64] = st_ref[...].astype(jnp.float32)
    twice[1:2, 64:128] = st_ref[...].astype(jnp.float32)
    sub = lax.broadcasted_iota(jnp.int32, (NZ, 128), 0)
    lane = lax.broadcasted_iota(jnp.int32, (NZ, 128), 1)
    here = jnp.logical_and(sub == z, lane // 64 == x % 2)
    for k in range(2):
        placed = jnp.where(here, twice[k : k + 1, :], 0.0)
        for cp in range(2):
            wt[2 * k + cp] = jnp.where(x // 2 == cp, placed, 0.0)

    mine.wait()
    pl.semaphore_wait(barrier, len(peers))

    pending = []

    def remote(src, dst, ssem, rsem, dev, keep=True):
        cp = pltpu.make_async_remote_copy(
            src_ref=src, dst_ref=dst, send_sem=ssem, recv_sem=rsem, device_id=dev, device_id_type=MESH
        )
        cp.start()
        if keep:
            pending.append(cp)
        return cp

    count = [0]

    def gsend(view, dev):
        k = count[0]
        count[0] += 1
        return remote(view, view, gs.at[k], gr.at[k], dev)

    columns = cand.shape[1]
    rows_dev = cand.shape[0]
    half = rows_dev // 2

    def chunk(dx, dz, first, last, side=0):
        xp, zp = xx(dx), zz(dz)
        rows = {0: pl.ds(0, rows_dev), 1: pl.ds(0, half), -1: pl.ds(half, half)}[side]
        return G.at[xp // 2, zp, xp % 2, rows, pl.ds(first, last - first)]

    def own_column(o):
        if o == 0:
            return []
        return [(ZB, 4, 1), (ZB, 4, -1)] if o == 4 else [(ZB, abs(o), -1 if o > 0 else 1)]

    def message(kind, *at):
        if kind == XA1:
            (s,) = at
            return chunk(0, 0, 0, CUT_OWN), xdev(s), []
        if kind == XA2:
            (s,) = at
            return chunk(-s, 0, 0, CUT_OWN, s), xdev(s), [(XA1, s)]
        if kind == ZB:
            d, s = at
            side = s if d == 4 else 0
            return chunk(0, -s * (d - 1), CUT_NEXT, columns, side), zdev(s), [(ZB, d - 1, s)] if d > 1 else []
        if kind == XB:
            o, s = at
            return chunk(0, o, CUT_NEXT if o else CUT_OWN, columns), xdev(s), own_column(o)
        if kind == XH:
            o, s = at
            return chunk(-s, o, CUT_FAR if o else CUT_OWN, columns, s), xdev(s), [(XB, o, s)]
        d, s, r = at
        first = {0: [], 1: [(XA1, -1)], -1: [(XA1, 1)], 2: [(XA2, 1), (XA2, -1)]}[r]
        after = [(ZA, d - 1, s, r)] if d > 1 else first
        return chunk(r, -s * (d - 1), 0, CUT_FAR if r == 2 else CUT_NEXT), zdev(s), after

    def whole(o):
        keys = [(kind, o, s) for kind in (XB, XH) for s in (1, -1)] + own_column(o)
        if o == 0:
            return keys + [(kind, s) for kind in (XA1, XA2) for s in (1, -1)]
        if o == 4:
            return keys + [(ZA, 4, 1, 0), (ZA, 4, 1, 1), (ZA, 4, -1, 2), (ZA, 4, -1, -1)]
        return keys + [(ZA, abs(o), -1 if o > 0 else 1, r) for r in (0, 1, -1, 2)]

    sent, received = {}, set()

    def receive(keys):
        for key in keys:
            if key not in received:
                received.add(key)
                sent[key].wait_recv()

    def product(o):
        zp = zz(o)
        a = G[:, zp].reshape(NX * rows_dev, cand.shape[1])
        for n in range(2):
            rows = pl.ds(n * 256, 256)
            p = lax.dot_general(
                F[rows, :], a, (((1,), (1,)), ((), ())), preferred_element_type=jnp.float32
            ).astype(jnp.bfloat16)
            pb[zp, 0, rows, :] = p[:, :128]
            pb[zp, 1, rows, :] = p[:, 128:]

    PX, YS = {}, {}

    def send_half(o):
        i = OFFSETS.index(o)
        zp = zz(o)
        PX[o] = remote(pb.at[zp, 1 - c], px.at[zp], pxs.at[i], pxr.at[i], fdev(0, 1))

    def send_quarters(o):
        i = OFFSETS.index(o)
        zp = zz(o)
        PX[o].wait_recv()
        q = pb[zp, c].astype(jnp.float32) + px[zp].astype(jnp.float32)
        ysb[zp] = q.astype(jnp.bfloat16).reshape(NY, 128, 128)
        for d in (2, 1, 3):
            yp = lax.rem(y + d, NY)
            YS[o, d] = remote(
                ysb.at[zp, yp], ysr.at[zp, d], yss.at[i * 3 + d - 1], ysrs.at[i * 3 + d - 1], fdev(d, 0)
            )

    def squares(o):
        zp = zz(o)
        total = ysb[zp, y].astype(jnp.float32)
        for d in range(1, NY):
            YS[o, d].wait_recv()
            total = total + ysr[zp, d].astype(jnp.float32)
        V[pl.ds(zp, 1), :] = jnp.sum(total * total, axis=0, keepdims=True)

    block = Ci.shape[-1]
    col0 = pl.multiple_of((z % 4) * block, block)
    croot = z // 4
    dy = lax.rem(y - x + NY, NY)
    on_core = c == croot
    is_root = jnp.logical_and(dy == 0, on_core)

    def ci_copy(o, slot, src, dev):
        i = OFFSETS.index(o)
        return pltpu.make_async_remote_copy(
            src_ref=src, dst_ref=Ci.at[:, zz(o)], send_sem=cs.at[i * 3 + slot], recv_sem=cr.at[i],
            device_id=dev, device_id_type=MESH,
        )

    def ci_source(o):
        return G.at[:, zz(o), :, :, pl.ds(col0, block)]

    def ci_root(o):
        @pl.when(is_root)
        def _():
            src = ci_source(o)
            ci_copy(o, 0, src, fdev(1, 0)).start()
            ci_copy(o, 1, src, fdev(3, 0)).start()
            ci_copy(o, 2, src, fdev(0, 1)).start()
            own = pltpu.make_async_copy(src, Ci.at[:, zz(o)], cr.at[OFFSETS.index(o)])
            own.start()
            own.wait()

    def ci_wait(o):
        ci_copy(o, 0, Ci.at[:, zz(o)], fdev(0, 1)).wait_recv()

    def ci_near(o):
        i = OFFSETS.index(o)
        for d in (1, 3):
            @pl.when(jnp.logical_and(on_core, dy == d))
            def _():
                ci_wait(o)
                if d == (1 if i % 2 == 0 else 3):
                    ci_copy(o, 0, Ci.at[:, zz(o)], fdev(d, 0)).start()
                ci_copy(o, 2, Ci.at[:, zz(o)], fdev(0, 1)).start()

    def ci_far(o):
        @pl.when(jnp.logical_and(on_core, dy == 2))
        def _():
            ci_wait(o)
            ci_copy(o, 2, Ci.at[:, zz(o)], fdev(0, 1)).start()

    def ci_last(o):
        @pl.when(jnp.logical_not(on_core))
        def _():
            ci_wait(o)

        for cp in range(2):
            t = Ci[cp, zz(o)].reshape(128, block)
            S[:, pl.ds(pl.multiple_of((cp * NZ + zz(o)) * 128, 128), 128)] = t.T

    def ci_finish(o):
        i = OFFSETS.index(o)

        @pl.when(is_root)
        def _():
            for slot in range(3):
                ci_copy(o, slot, ci_source(o), fdev(0, 1)).wait_send()

        for d in (1, 2, 3):
            @pl.when(jnp.logical_and(on_core, dy == d))
            def _():
                if d == (1 if i % 2 == 0 else 3):
                    ci_copy(o, 0, Ci.at[:, zz(o)], fdev(0, 1)).wait_send()
                ci_copy(o, 2, Ci.at[:, zz(o)], fdev(0, 1)).wait_send()

    WX, WZ = [], []
    near, far = [], []
    for op in ORDER:
        kind, at = op[0], op[1:]
        if kind <= ZA:
            view, dev, after = message(*op)
            receive(after)
            sent[op] = gsend(view, dev)
        elif kind == PRODUCT:
            (o,) = at
            receive(whole(o))
            if o == 0:
                fcopy.wait()
            if o != 4:
                ci_root(o)
            product(o)
            send_half(o)
            if o == 0:
                WX = [remote(wt, wx.at[d], ws.at[d - 1], wr.at[d - 1], xdev(d)) for d in range(1, NX)]
            if o == -2:
                total = wt[...]
                for d in range(1, NX):
                    WX[d - 1].wait_recv()
                    total = total + wx[d]
                wz0[...] = total
                receive(own_column(4))
                WZ = [remote(wz0, wz.at[d], ws.at[d + 2], wr.at[d + 2], zdev(d)) for d in range(1, NZ)]
        elif kind == QUARTERS:
            send_quarters(*at)
            if at == (4,):
                ci_root(4)
                for o in OFFSETS[:-1]:
                    if o not in near:
                        ci_near(o)
                        near.append(o)
                last = list(far)
                for o in last:
                    ci_last(o)
        elif kind == SQUARES:
            squares(*at)
        elif kind == NEAR:
            ci_near(*at)
            near += at
        else:
            ci_far(*at)
            far += at

    lz0[...] = V[...]
    for k, (dx, dz) in enumerate(plane_peers):
        remote(lz0, lz.at[k], ls.at[0], lr.at[0], (xx(dx) * NZ + zz(dz), feat), keep=False)
    all_sums = pltpu.make_async_remote_copy(
        src_ref=lz, dst_ref=lz, send_sem=ls.at[0], recv_sem=lr.at[0], device_id=xdev(1), device_id_type=MESH
    )
    ci_near(4)
    for o in OFFSETS[:-1]:
        if o not in far:
            ci_far(o)
            far.append(o)
    total = wz0[...]
    for d in range(1, NZ):
        WZ[d - 1].wait_recv()
        total = total + wz[d]
    wz0_all = total
    v = lz0[...]
    all_sums.wait_recv()
    for k in range(len(plane_peers)):
        v = v + lz[k]
    lt0[...] = v
    LT = [
        remote(lt0, lt.at[k], ls.at[k + 9], lr.at[k + 9], fdev(*d)) for k, d in enumerate(fcopies, 1)
    ]
    weights = [wz0_all[0], wz0_all[1]]
    labels = [wz0_all[2], wz0_all[3]]
    ids = lax.broadcasted_iota(jnp.int32, (STRATA, 128), 0).astype(jnp.float32)

    def over_strata(tiles):
        acc = jnp.zeros((STRATA, 128), jnp.float32)
        for cp in range(2):
            for zp in range(NZ):
                acc = acc + jnp.where(labels[cp][zp : zp + 1, :] == ids, tiles[cp][zp : zp + 1, :], 0.0)
        return jnp.sum(acc, axis=1, keepdims=True)

    mass = over_strata(weights)
    all_sums.wait_send()
    for o in OFFSETS:
        if o not in far:
            ci_far(o)
    for o in OFFSETS:
        if o not in last:
            ci_last(o)
    for cp in pending:
        cp.wait_send()
    for o in OFFSETS:
        ci_finish(o)
    same, other = lt0[...], None
    for k, (dyk, dck) in enumerate(fcopies, 1):
        LT[k - 1].wait_recv()
        if dck == 0:
            same = same + lt[k]
        else:
            other = lt[k] if other is None else other + lt[k]
    first = c == 0
    raw = [jnp.where(first, same, other), jnp.where(first, other, same)]
    products = [weights[cp] * raw[cp] for cp in range(2)]
    ratio = mass / over_strata(products)
    new_weights = []
    for cp in range(2):
        rows = [
            jnp.sum(jnp.where(labels[cp][zp : zp + 1, :] == ids, ratio, 0.0), axis=0, keepdims=True)
            for zp in range(NZ)
        ]
        row_ratio = jnp.concatenate(rows, axis=0)
        new_weight = products[cp] * row_ratio
        new_weights.append(new_weight)
        step = new_weight - weights[cp]
        for zp in range(NZ):
            cols = pl.ds((cp * NZ + zp) * 128, 128)
            S[:, cols] = (S[:, cols].astype(jnp.float32) * step[zp : zp + 1, :]).astype(jnp.bfloat16)

    def own_rows(tiles):
        tile = jnp.where(x // 2 == 0, tiles[0], tiles[1])
        line = jnp.sum(jnp.where(sub == z, tile, 0.0), axis=0, keepdims=True)
        return jnp.where(x % 2 == 0, line[:, :64], line[:, 64:])

    nw_ref[...] = own_rows(new_weights)
    lev_ref[...] = own_rows(raw) / features


def gather(cand, fac, weights, strata):
    rows_dev, feat_block = cand.shape
    row_block = fac.shape[0]
    bf, f32 = jnp.bfloat16, jnp.float32
    vmem = pl.BlockSpec(memory_space=pltpu.VMEM)
    hbm = pl.BlockSpec(memory_space=pltpu.HBM)
    dma = pltpu.SemaphoreType.DMA
    return pl.pallas_call(
        gather_kernel,
        out_shape=(
            pltpu.VMEM((2, NZ, 2, rows_dev, feat_block), bf),
            pltpu.VMEM((row_block, NX * NZ * rows_dev), bf),
            pltpu.VMEM((1, rows_dev), f32),
            pltpu.VMEM((1, rows_dev), f32),
        ),
        in_specs=[hbm, hbm, hbm, hbm],
        out_specs=(vmem, vmem, vmem, vmem),
        scratch_shapes=[
            pltpu.VMEM((1, rows_dev), f32),
            pltpu.VMEM((1, rows_dev), jnp.int32),
            pltpu.VMEM((8, 128), f32),
            pltpu.VMEM((4, NZ, 128), f32),
            pltpu.VMEM(fac.shape, bf),
            pltpu.VMEM((2, NZ, 2, rows_dev, row_block), bf),
            pltpu.VMEM((NZ, 2, row_block, 128), bf),
            pltpu.VMEM((NZ, row_block, 128), bf),
            pltpu.VMEM((NZ, NY, 128, 128), bf),
            pltpu.VMEM((NZ, NY, 128, 128), bf),
            pltpu.VMEM((NZ, 128), f32),
            pltpu.VMEM((NX, 4, NZ, 128), f32),
            pltpu.VMEM((4, NZ, 128), f32),
            pltpu.VMEM((NZ, 4, NZ, 128), f32),
            pltpu.VMEM((NZ, 128), f32),
            pltpu.VMEM((NX * NZ - 1, NZ, 128), f32),
            pltpu.VMEM((NZ, 128), f32),
            pltpu.VMEM((NZ, NZ, 128), f32),
            dma((4,)),
            dma((72,)),
            dma((72,)),
            dma((10,)),
            dma((10,)),
            dma((8,)),
            dma((8,)),
            dma((24,)),
            dma((24,)),
            dma((24,)),
            dma((8,)),
            dma((17,)),
            dma((17,)),
        ],
        compiler_params=pltpu.CompilerParams(
            collective_id=0, has_side_effects=True, vmem_limit_bytes=40 * 1024 * 1024
        ),
    )(*[
        pltpu.with_memory_space_constraint(a, pltpu.HBM)
        for a in (cand, fac, weights.reshape(1, rows_dev), strata.reshape(1, rows_dev))
    ])


WIDTH = 512


def increment_kernel(s_ref, g_ref, nw_ref, lev_ref, o_hbm, nw_hbm, lev_hbm, out, sem):
    copies = [
        pltpu.make_async_copy(nw_ref, nw_hbm, sem.at[0]),
        pltpu.make_async_copy(lev_ref, lev_hbm, sem.at[1]),
    ]
    for cp in copies:
        cp.start()
    for j in range(out.shape[1] // WIDTH):
        cols = pl.ds(j * WIDTH, WIDTH)
        out[:, cols] = jnp.dot(s_ref[...], g_ref[:, cols], preferred_element_type=jnp.float32)
        cp = pltpu.make_async_copy(out.at[:, cols], o_hbm.at[:, cols], sem.at[2 + j])
        cp.start()
        copies.append(cp)
    for cp in copies:
        cp.wait()


def increment(s, g, nw, lev):
    rows = s.shape[0]
    columns = g.shape[1]
    vmem = pl.BlockSpec(memory_space=pltpu.VMEM)
    hbm = pl.BlockSpec(memory_space=pltpu.HBM)
    f32 = jnp.float32
    return pl.pallas_call(
        increment_kernel,
        out_shape=(pltpu.HBM((rows, columns), f32), pltpu.HBM(nw.shape, f32), pltpu.HBM(lev.shape, f32)),
        in_specs=[vmem] * 4,
        out_specs=(hbm,) * 3,
        scratch_shapes=[
            pltpu.VMEM((rows, columns), f32),
            pltpu.SemaphoreType.DMA((2 + columns // WIDTH,)),
        ],
        compiler_params=pltpu.CompilerParams(vmem_limit_bytes=30 * 1024 * 1024),
    )(s, g, nw, lev)


def per_device(candidates, inv_factor, weights, strata):
    g, s, nw, lev = gather(candidates, inv_factor, weights, strata)
    information, nw, lev = increment(s, g.reshape(-1, g.shape[-1]), nw, lev)
    return (nw.reshape(weights.shape), lev.reshape(weights.shape), information)


def solution(mesh):
    in_specs = (P("row", "feat"), P("row", "feat"), P("row"), P("row"))
    out_specs = (P("row"), P("row"), P("row", "feat"))
    return jax.shard_map(
        per_device, mesh=mesh, in_specs=in_specs, out_specs=out_specs, check_vma=False
    )
```

```python
import functools

import jax
import jax.numpy as jnp
from jax import lax
from jax.experimental import pallas as pl
from jax.experimental.pallas import tpu as pltpu
from jax.sharding import PartitionSpec as P

MESH = pl.DeviceIdType.MESH
NX, NY, NZ, NC = 4, 4, 8, 2
STRATA = 64
OFFSETS = (0, 1, -1, 2, -2, 3, -3, 4)
CUT_OWN, CUT_NEXT, CUT_FAR = 896, 768, 896
XA1, XA2, ZB, XB, XH, ZA, PRODUCT, QUARTERS, SQUARES, NEAR, FAR = range(11)
ORDER = (
    (ZB, 1, -1), (ZB, 1, 1), (XA1, -1), (XA1, 1), (XB, 0, -1), (XB, 0, 1), (ZA, 1, -1, 0), (ZA, 1, 1, 0),
    (XA2, -1), (ZA, 1, -1, 1), (XA2, 1), (ZA, 1, 1, 1), (XB, 1, -1), (XB, 1, 1), (ZB, 2, -1), (ZB, 2, 1),
    (XH, 0, -1), (XH, 0, 1), (ZA, 1, -1, -1), (ZA, 1, 1, -1), (XB, -1, -1), (XB, -1, 1), (ZA, 1, -1, 2),
    (ZA, 1, 1, 2), (XH, 1, -1), (XH, 1, 1), (ZB, 3, -1), (ZB, 3, 1), (PRODUCT, 0), (XB, 2, -1), (XB, 2, 1),
    (QUARTERS, 0), (ZA, 2, -1, 0), (ZA, 2, 1, 0), (XH, -1, -1), (XH, -1, 1), (PRODUCT, 1), (ZA, 2, -1, 1),
    (ZA, 2, 1, 1), (XB, -2, -1), (XB, -2, 1), (SQUARES, 0), (QUARTERS, 1), (ZB, 4, -1), (ZB, 4, 1), (NEAR, 0),
    (ZA, 2, -1, -1), (ZA, 2, 1, -1), (XH, 2, -1), (XH, 2, 1), (PRODUCT, -1), (ZA, 2, -1, 2), (ZA, 2, 1, 2),
    (XB, 3, -1), (XB, 3, 1), (SQUARES, 1), (QUARTERS, -1), (NEAR, 1), (ZA, 3, -1, 0), (ZA, 3, 1, 0),
    (XH, -2, -1), (XH, -2, 1), (SQUARES, -1), (ZA, 3, -1, 1), (ZA, 3, 1, 1), (XB, -3, -1), (XB, -3, 1),
    (PRODUCT, 2), (ZA, 3, -1, -1), (ZA, 3, 1, -1), (FAR, 0), (NEAR, -1), (QUARTERS, 2), (XH, 3, -1),
    (XH, 3, 1), (ZA, 3, -1, 2), (ZA, 3, 1, 2), (PRODUCT, -2), (XB, 4, -1), (XB, 4, 1), (QUARTERS, -2),
    (ZA, 4, 1, 0), (FAR, 1), (SQUARES, 2), (ZA, 4, -1, -1), (ZA, 4, 1, 1), (XH, -3, -1), (XH, -3, 1),
    (SQUARES, -2), (NEAR, 2), (ZA, 4, -1, 2), (PRODUCT, 3), (QUARTERS, 3), (FAR, -1), (NEAR, -2), (XH, 4, -1),
    (XH, 4, 1), (PRODUCT, -3), (SQUARES, 3), (QUARTERS, -3), (PRODUCT, 4), (QUARTERS, 4), (SQUARES, -3),
    (SQUARES, 4),
)


def gather_kernel(
    cand, fac, w_hbm, st_hbm,
    G, S, nw_ref, lev_ref,
    w_ref, st_ref, twice, wt, F, Ci, pb, px, ysb, ysr, V, wx, wz0, wz, lz0, lz, lt0, lt,
    loc_sem, gs, gr, ws, wr, pxs, pxr, yss, ysrs, cs, cr, ls, lr,
):
    features = NY * NC * cand.shape[1]
    row, feat = lax.axis_index("row"), lax.axis_index("feat")
    x, z = row // NZ, row % NZ
    y, c = feat // NC, feat % NC

    def xdev(d):
        return (lax.rem(x + d + NX, NX) * NZ + z, feat)

    def zdev(d):
        return (x * NZ + lax.rem(z + d + NZ, NZ), feat)

    def fdev(dy, dc):
        return (row, lax.rem(y + dy, NY) * NC + lax.rem(c + dc, NC))

    plane_peers = sorted(
        ((dx, dz) for dx in range(NX) for dz in range(NZ) if (dx, dz) != (0, 0)),
        key=lambda d: -(min(d[0], NX - d[0]) + min(d[1], NZ - d[1])),
    )
    fcopies = [(dy, dc) for dy in (2, 1, 3, 0) for dc in range(NC) if (dy, dc) != (0, 0)]

    def xx(d):
        return lax.rem(x + d + NX, NX)

    def zz(d):
        return lax.rem(z + d + NZ, NZ)

    fcopy = pltpu.make_async_copy(fac, F, loc_sem.at[0])
    smalls = [
        pltpu.make_async_copy(w_hbm, w_ref, loc_sem.at[2]),
        pltpu.make_async_copy(st_hbm, st_ref, loc_sem.at[3]),
    ]
    mine = pltpu.make_async_copy(cand, G.at[x // 2, z, x % 2], loc_sem.at[1])
    mine.start()
    for cp in smalls:
        cp.start()
    fcopy.start()

    barrier = pltpu.get_barrier_semaphore()
    peers = [xdev(1), xdev(-1), zdev(1), zdev(-1), fdev(0, 1)] + [fdev(d, 0) for d in range(1, NY)]
    for dev in peers:
        pl.semaphore_signal(barrier, inc=1, device_id=dev, device_id_type=MESH)
    for cp in smalls:
        cp.wait()
    twice[0:1, 0:64] = w_ref[...]
    twice[0:1, 64:128] = w_ref[...]
    twice[1:2, 0:64] = st_ref[...].astype(jnp.float32)
    twice[1:2, 64:128] = st_ref[...].astype(jnp.float32)
    sub = lax.broadcasted_iota(jnp.int32, (NZ, 128), 0)
    lane = lax.broadcasted_iota(jnp.int32, (NZ, 128), 1)
    here = jnp.logical_and(sub == z, lane // 64 == x % 2)
    for k in range(2):
        placed = jnp.where(here, twice[k : k + 1, :], 0.0)
        for cp in range(2):
            wt[2 * k + cp] = jnp.where(x // 2 == cp, placed, 0.0)

    mine.wait()
    pl.semaphore_wait(barrier, len(peers))

    pending = []

    def remote(src, dst, ssem, rsem, dev, keep=True):
        cp = pltpu.make_async_remote_copy(
            src_ref=src, dst_ref=dst, send_sem=ssem, recv_sem=rsem, device_id=dev, device_id_type=MESH
        )
        cp.start()
        if keep:
            pending.append(cp)
        return cp

    count = [0]

    def gsend(view, dev):
        k = count[0]
        count[0] += 1
        return remote(view, view, gs.at[k], gr.at[k], dev)

    columns = cand.shape[1]
    rows_dev = cand.shape[0]
    half = rows_dev // 2

    def chunk(dx, dz, first, last, side=0):
        xp, zp = xx(dx), zz(dz)
        rows = {0: pl.ds(0, rows_dev), 1: pl.ds(0, half), -1: pl.ds(half, half)}[side]
        return G.at[xp // 2, zp, xp % 2, rows, pl.ds(first, last - first)]

    def own_column(o):
        if o == 0:
            return []
        return [(ZB, 4, 1), (ZB, 4, -1)] if o == 4 else [(ZB, abs(o), -1 if o > 0 else 1)]

    def message(kind, *at):
        if kind == XA1:
            (s,) = at
            return chunk(0, 0, 0, CUT_OWN), xdev(s), []
        if kind == XA2:
            (s,) = at
            return chunk(-s, 0, 0, CUT_OWN, s), xdev(s), [(XA1, s)]
        if kind == ZB:
            d, s = at
            side = s if d == 4 else 0
            return chunk(0, -s * (d - 1), CUT_NEXT, columns, side), zdev(s), [(ZB, d - 1, s)] if d > 1 else []
        if kind == XB:
            o, s = at
            return chunk(0, o, CUT_NEXT if o else CUT_OWN, columns), xdev(s), own_column(o)
        if kind == XH:
            o, s = at
            return chunk(-s, o, CUT_FAR if o else CUT_OWN, columns, s), xdev(s), [(XB, o, s)]
        d, s, r = at
        first = {0: [], 1: [(XA1, -1)], -1: [(XA1, 1)], 2: [(XA2, 1), (XA2, -1)]}[r]
        after = [(ZA, d - 1, s, r)] if d > 1 else first
        return chunk(r, -s * (d - 1), 0, CUT_FAR if r == 2 else CUT_NEXT), zdev(s), after

    def whole(o):
        keys = [(kind, o, s) for kind in (XB, XH) for s in (1, -1)] + own_column(o)
        if o == 0:
            return keys + [(kind, s) for kind in (XA1, XA2) for s in (1, -1)]
        if o == 4:
            return keys + [(ZA, 4, 1, 0), (ZA, 4, 1, 1), (ZA, 4, -1, 2), (ZA, 4, -1, -1)]
        return keys + [(ZA, abs(o), -1 if o > 0 else 1, r) for r in (0, 1, -1, 2)]

    sent, received = {}, set()

    def receive(keys):
        for key in keys:
            if key not in received:
                received.add(key)
                sent[key].wait_recv()

    def product(o):
        zp = zz(o)
        a = G[:, zp].reshape(NX * rows_dev, cand.shape[1])
        for n in range(2):
            rows = pl.ds(n * 256, 256)
            p = lax.dot_general(
                F[rows, :], a, (((1,), (1,)), ((), ())), preferred_element_type=jnp.float32
            ).astype(jnp.bfloat16)
            pb[zp, 0, rows, :] = p[:, :128]
            pb[zp, 1, rows, :] = p[:, 128:]

    PX, YS = {}, {}

    def send_half(o):
        i = OFFSETS.index(o)
        zp = zz(o)
        PX[o] = remote(pb.at[zp, 1 - c], px.at[zp], pxs.at[i], pxr.at[i], fdev(0, 1))

    def send_quarters(o):
        i = OFFSETS.index(o)
        zp = zz(o)
        PX[o].wait_recv()
        q = pb[zp, c].astype(jnp.float32) + px[zp].astype(jnp.float32)
        ysb[zp] = q.astype(jnp.bfloat16).reshape(NY, 128, 128)
        for d in (2, 1, 3):
            yp = lax.rem(y + d, NY)
            YS[o, d] = remote(
                ysb.at[zp, yp], ysr.at[zp, d], yss.at[i * 3 + d - 1], ysrs.at[i * 3 + d - 1], fdev(d, 0)
            )

    def squares(o):
        zp = zz(o)
        total = ysb[zp, y].astype(jnp.float32)
        for d in range(1, NY):
            YS[o, d].wait_recv()
            total = total + ysr[zp, d].astype(jnp.float32)
        V[pl.ds(zp, 1), :] = jnp.sum(total * total, axis=0, keepdims=True)

    block = Ci.shape[-1]
    col0 = pl.multiple_of((z % 4) * block, block)
    croot = z // 4
    dy = lax.rem(y - x + NY, NY)
    on_core = c == croot
    is_root = jnp.logical_and(dy == 0, on_core)

    def ci_copy(o, slot, src, dev):
        i = OFFSETS.index(o)
        return pltpu.make_async_remote_copy(
            src_ref=src, dst_ref=Ci.at[:, zz(o)], send_sem=cs.at[i * 3 + slot], recv_sem=cr.at[i],
            device_id=dev, device_id_type=MESH,
        )

    def ci_source(o):
        return G.at[:, zz(o), :, :, pl.ds(col0, block)]

    def ci_root(o):
        @pl.when(is_root)
        def _():
            src = ci_source(o)
            ci_copy(o, 0, src, fdev(1, 0)).start()
            ci_copy(o, 1, src, fdev(3, 0)).start()
            ci_copy(o, 2, src, fdev(0, 1)).start()
            own = pltpu.make_async_copy(src, Ci.at[:, zz(o)], cr.at[OFFSETS.index(o)])
            own.start()
            own.wait()

    def ci_wait(o):
        ci_copy(o, 0, Ci.at[:, zz(o)], fdev(0, 1)).wait_recv()

    def ci_near(o):
        i = OFFSETS.index(o)
        for d in (1, 3):
            @pl.when(jnp.logical_and(on_core, dy == d))
            def _():
                ci_wait(o)
                if d == (1 if i % 2 == 0 else 3):
                    ci_copy(o, 0, Ci.at[:, zz(o)], fdev(d, 0)).start()
                ci_copy(o, 2, Ci.at[:, zz(o)], fdev(0, 1)).start()

    def ci_far(o):
        @pl.when(jnp.logical_and(on_core, dy == 2))
        def _():
            ci_wait(o)
            ci_copy(o, 2, Ci.at[:, zz(o)], fdev(0, 1)).start()

    def ci_last(o):
        @pl.when(jnp.logical_not(on_core))
        def _():
            ci_wait(o)

        for cp in range(2):
            t = Ci[cp, zz(o)].reshape(128, block)
            S[:, pl.ds(pl.multiple_of((cp * NZ + zz(o)) * 128, 128), 128)] = t.T

    def ci_finish(o):
        i = OFFSETS.index(o)

        @pl.when(is_root)
        def _():
            for slot in range(3):
                ci_copy(o, slot, ci_source(o), fdev(0, 1)).wait_send()

        for d in (1, 2, 3):
            @pl.when(jnp.logical_and(on_core, dy == d))
            def _():
                if d == (1 if i % 2 == 0 else 3):
                    ci_copy(o, 0, Ci.at[:, zz(o)], fdev(0, 1)).wait_send()
                ci_copy(o, 2, Ci.at[:, zz(o)], fdev(0, 1)).wait_send()

    WX, WZ = [], []
    near, far = [], []
    for op in ORDER:
        kind, at = op[0], op[1:]
        if kind <= ZA:
            view, dev, after = message(*op)
            receive(after)
            sent[op] = gsend(view, dev)
        elif kind == PRODUCT:
            (o,) = at
            receive(whole(o))
            if o == 0:
                fcopy.wait()
            if o != 4:
                ci_root(o)
            product(o)
            send_half(o)
            if o == 0:
                WX = [remote(wt, wx.at[d], ws.at[d - 1], wr.at[d - 1], xdev(d)) for d in range(1, NX)]
            if o == -2:
                total = wt[...]
                for d in range(1, NX):
                    WX[d - 1].wait_recv()
                    total = total + wx[d]
                wz0[...] = total
                receive(own_column(4))
                WZ = [remote(wz0, wz.at[d], ws.at[d + 2], wr.at[d + 2], zdev(d)) for d in range(1, NZ)]
        elif kind == QUARTERS:
            send_quarters(*at)
            if at == (4,):
                ci_root(4)
                for o in OFFSETS[:-1]:
                    if o not in near:
                        ci_near(o)
                        near.append(o)
                last = list(far)
                for o in last:
                    ci_last(o)
        elif kind == SQUARES:
            squares(*at)
        elif kind == NEAR:
            ci_near(*at)
            near += at
        else:
            ci_far(*at)
            far += at

    lz0[...] = V[...]
    for k, (dx, dz) in enumerate(plane_peers):
        remote(lz0, lz.at[k], ls.at[0], lr.at[0], (xx(dx) * NZ + zz(dz), feat), keep=False)
    all_sums = pltpu.make_async_remote_copy(
        src_ref=lz, dst_ref=lz, send_sem=ls.at[0], recv_sem=lr.at[0], device_id=xdev(1), device_id_type=MESH
    )
    ci_near(4)
    for o in OFFSETS[:-1]:
        if o not in far:
            ci_far(o)
            far.append(o)
    total = wz0[...]
    for d in range(1, NZ):
        WZ[d - 1].wait_recv()
        total = total + wz[d]
    weights, labels = [total[0], total[1]], [total[2], total[3]]
    ids = lax.broadcasted_iota(jnp.int32, (STRATA, 128), 0).astype(jnp.float32)

    def over_strata(tiles):
        acc = jnp.zeros((STRATA, 128), jnp.float32)
        for cp in range(2):
            for zp in range(NZ):
                acc = acc + jnp.where(labels[cp][zp : zp + 1, :] == ids, tiles[cp][zp : zp + 1, :], 0.0)
        return jnp.sum(acc, axis=1, keepdims=True)

    mass = over_strata(weights)
    for cp in pending:
        cp.wait_send()
    late = OFFSETS[-3:]
    for o in OFFSETS:
        if o not in last and o not in late:
            ci_last(o)
    v = lz0[...]
    all_sums.wait_recv()
    for k in range(len(plane_peers)):
        v = v + lz[k]
    lt0[...] = v
    LT = [
        remote(lt0, lt.at[k], ls.at[k + 9], lr.at[k + 9], fdev(*d), keep=False)
        for k, d in enumerate(fcopies, 1)
    ]
    all_sums.wait_send()
    ci_far(4)
    for o in late:
        ci_last(o)
    for o in OFFSETS:
        ci_finish(o)
    same, other = lt0[...], None
    for k, (dyk, dck) in enumerate(fcopies, 1):
        LT[k - 1].wait_recv()
        if dck == 0:
            same = same + lt[k]
        else:
            other = lt[k] if other is None else other + lt[k]
    first = c == 0
    raw = [jnp.where(first, same, other), jnp.where(first, other, same)]
    products = [weights[cp] * raw[cp] for cp in range(2)]
    ratio = mass / over_strata(products)
    new_weights = []
    for cp in range(2):
        rows = [
            jnp.sum(jnp.where(labels[cp][zp : zp + 1, :] == ids, ratio, 0.0), axis=0, keepdims=True)
            for zp in range(NZ)
        ]
        row_ratio = jnp.concatenate(rows, axis=0)
        new_weight = products[cp] * row_ratio
        new_weights.append(new_weight)
        step = new_weight - weights[cp]
        for zp in range(NZ):
            cols = pl.ds((cp * NZ + zp) * 128, 128)
            S[:, cols] = (S[:, cols].astype(jnp.float32) * step[zp : zp + 1, :]).astype(jnp.bfloat16)

    def own_rows(tiles):
        tile = jnp.where(x // 2 == 0, tiles[0], tiles[1])
        line = jnp.sum(jnp.where(sub == z, tile, 0.0), axis=0, keepdims=True)
        return jnp.where(x % 2 == 0, line[:, :64], line[:, 64:])

    nw_ref[...] = own_rows(new_weights)
    lev_ref[...] = own_rows(raw) / features
    for cp in LT:
        cp.wait_send()


def gather(cand, fac, weights, strata):
    rows_dev, feat_block = cand.shape
    row_block = fac.shape[0]
    bf, f32 = jnp.bfloat16, jnp.float32
    vmem = pl.BlockSpec(memory_space=pltpu.VMEM)
    hbm = pl.BlockSpec(memory_space=pltpu.HBM)
    dma = pltpu.SemaphoreType.DMA
    return pl.pallas_call(
        gather_kernel,
        out_shape=(
            pltpu.VMEM((2, NZ, 2, rows_dev, feat_block), bf),
            pltpu.VMEM((row_block, NX * NZ * rows_dev), bf),
            pltpu.VMEM((1, rows_dev), f32),
            pltpu.VMEM((1, rows_dev), f32),
        ),
        in_specs=[hbm, hbm, hbm, hbm],
        out_specs=(vmem, vmem, vmem, vmem),
        scratch_shapes=[
            pltpu.VMEM((1, rows_dev), f32),
            pltpu.VMEM((1, rows_dev), jnp.int32),
            pltpu.VMEM((8, 128), f32),
            pltpu.VMEM((4, NZ, 128), f32),
            pltpu.VMEM(fac.shape, bf),
            pltpu.VMEM((2, NZ, 2, rows_dev, row_block), bf),
            pltpu.VMEM((NZ, 2, row_block, 128), bf),
            pltpu.VMEM((NZ, row_block, 128), bf),
            pltpu.VMEM((NZ, NY, 128, 128), bf),
            pltpu.VMEM((NZ, NY, 128, 128), bf),
            pltpu.VMEM((NZ, 128), f32),
            pltpu.VMEM((NX, 4, NZ, 128), f32),
            pltpu.VMEM((4, NZ, 128), f32),
            pltpu.VMEM((NZ, 4, NZ, 128), f32),
            pltpu.VMEM((NZ, 128), f32),
            pltpu.VMEM((NX * NZ - 1, NZ, 128), f32),
            pltpu.VMEM((NZ, 128), f32),
            pltpu.VMEM((NZ, NZ, 128), f32),
            dma((4,)),
            dma((72,)),
            dma((72,)),
            dma((10,)),
            dma((10,)),
            dma((8,)),
            dma((8,)),
            dma((24,)),
            dma((24,)),
            dma((24,)),
            dma((8,)),
            dma((17,)),
            dma((17,)),
        ],
        compiler_params=pltpu.CompilerParams(
            collective_id=0, has_side_effects=True, vmem_limit_bytes=40 * 1024 * 1024
        ),
    )(*[
        pltpu.with_memory_space_constraint(a, pltpu.HBM)
        for a in (cand, fac, weights.reshape(1, rows_dev), strata.reshape(1, rows_dev))
    ])


WIDTH = 512


def increment_kernel(s_ref, g_ref, nw_ref, lev_ref, o_hbm, nw_hbm, lev_hbm, out, sem):
    copies = [
        pltpu.make_async_copy(nw_ref, nw_hbm, sem.at[0]),
        pltpu.make_async_copy(lev_ref, lev_hbm, sem.at[1]),
    ]
    for cp in copies:
        cp.start()
    for j in range(out.shape[1] // WIDTH):
        cols = pl.ds(j * WIDTH, WIDTH)
        out[:, cols] = jnp.dot(s_ref[...], g_ref[:, cols], preferred_element_type=jnp.float32)
        cp = pltpu.make_async_copy(out.at[:, cols], o_hbm.at[:, cols], sem.at[2 + j])
        cp.start()
        copies.append(cp)
    for cp in copies:
        cp.wait()


def increment(s, g, nw, lev):
    rows = s.shape[0]
    columns = g.shape[1]
    vmem = pl.BlockSpec(memory_space=pltpu.VMEM)
    hbm = pl.BlockSpec(memory_space=pltpu.HBM)
    f32 = jnp.float32
    return pl.pallas_call(
        increment_kernel,
        out_shape=(pltpu.HBM((rows, columns), f32), pltpu.HBM(nw.shape, f32), pltpu.HBM(lev.shape, f32)),
        in_specs=[vmem] * 4,
        out_specs=(hbm,) * 3,
        scratch_shapes=[
            pltpu.VMEM((rows, columns), f32),
            pltpu.SemaphoreType.DMA((2 + columns // WIDTH,)),
        ],
        compiler_params=pltpu.CompilerParams(vmem_limit_bytes=30 * 1024 * 1024),
    )(s, g, nw, lev)


def per_device(candidates, inv_factor, weights, strata):
    g, s, nw, lev = gather(candidates, inv_factor, weights, strata)
    information, nw, lev = increment(s, g.reshape(-1, g.shape[-1]), nw, lev)
    return (nw.reshape(weights.shape), lev.reshape(weights.shape), information)


def solution(mesh):
    in_specs = (P("row", "feat"), P("row", "feat"), P("row"), P("row"))
    out_specs = (P("row"), P("row"), P("row", "feat"))
    return jax.shard_map(
        per_device, mesh=mesh, in_specs=in_specs, out_specs=out_specs, check_vma=False
    )
```

```python
import functools

import jax
import jax.numpy as jnp
from jax import lax
from jax.experimental import pallas as pl
from jax.experimental.pallas import tpu as pltpu
from jax.sharding import PartitionSpec as P

MESH = pl.DeviceIdType.MESH
NX, NY, NZ, NC = 4, 4, 8, 2
STRATA = 64
OFFSETS = (0, 1, -1, 2, -2, 3, -3, 4)
CUT_OWN, CUT_NEXT, CUT_FAR = 896, 768, 896
XA1, XA2, ZB, XB, XH, ZA, PRODUCT, QUARTERS, SQUARES, NEAR, FAR = range(11)
ORDER = (
    (ZB, 1, -1), (ZB, 1, 1), (XA1, -1), (XA1, 1), (XB, 0, -1), (XB, 0, 1), (ZA, 1, -1, 0), (ZA, 1, 1, 0),
    (XA2, -1), (ZA, 1, -1, 1), (XA2, 1), (ZA, 1, 1, 1), (ZA, 1, -1, -1), (ZA, 1, 1, -1), (XB, 1, -1),
    (XB, 1, 1), (ZB, 2, -1), (ZB, 2, 1), (XH, 0, -1), (XH, 0, 1), (XB, -1, -1), (XB, -1, 1), (ZA, 1, -1, 2),
    (ZA, 1, 1, 2), (XH, 1, -1), (XH, 1, 1), (ZA, 2, -1, 0), (ZA, 2, 1, 0), (PRODUCT, 0), (XB, 2, -1),
    (XB, 2, 1), (ZB, 3, -1), (ZB, 3, 1), (QUARTERS, 0), (XH, -1, -1), (XH, -1, 1), (ZA, 2, -1, 1),
    (ZA, 2, 1, 1), (PRODUCT, 1), (XB, -2, -1), (XB, -2, 1), (SQUARES, 0), (QUARTERS, 1), (ZA, 2, -1, -1),
    (ZA, 2, 1, -1), (NEAR, 0), (ZA, 2, -1, 2), (ZA, 2, 1, 2), (XH, 2, -1), (XH, 2, 1), (PRODUCT, -1),
    (XB, 3, -1), (XB, 3, 1), (SQUARES, 1), (ZB, 4, -1), (ZB, 4, 1), (QUARTERS, -1), (ZA, 3, -1, 0),
    (ZA, 3, 1, 0), (NEAR, 1), (XH, -2, -1), (XH, -2, 1), (SQUARES, -1), (ZA, 3, -1, 1), (ZA, 3, 1, 1),
    (PRODUCT, 2), (XB, -3, -1), (XB, -3, 1), (ZA, 3, -1, -1), (ZA, 3, 1, -1), (FAR, 0), (QUARTERS, 2),
    (NEAR, -1), (XH, 3, -1), (XH, 3, 1), (ZA, 3, -1, 2), (ZA, 3, 1, 2), (PRODUCT, -2), (XB, 4, -1),
    (XB, 4, 1), (SQUARES, 2), (QUARTERS, -2), (ZA, 4, 1, 0), (FAR, 1), (ZA, 4, -1, -1), (ZA, 4, 1, 1),
    (NEAR, 2), (XH, -3, -1), (XH, -3, 1), (SQUARES, -2), (ZA, 4, -1, 2), (PRODUCT, 3), (FAR, -1),
    (QUARTERS, 3), (NEAR, -2), (XH, 4, -1), (XH, 4, 1), (PRODUCT, -3), (SQUARES, 3), (QUARTERS, -3),
    (PRODUCT, 4), (QUARTERS, 4), (SQUARES, -3), (SQUARES, 4),
)


def gather_kernel(
    cand, fac, w_hbm, st_hbm,
    G, S, nw_ref, lev_ref,
    w_ref, st_ref, twice, wt, F, Ci, pb, px, ysb, ysr, V, wx, wz0, wz, lz0, lz, lt0, lt,
    loc_sem, gs, gr, ws, wr, pxs, pxr, yss, ysrs, cs, cr, ls, lr,
):
    features = NY * NC * cand.shape[1]
    row, feat = lax.axis_index("row"), lax.axis_index("feat")
    x, z = row // NZ, row % NZ
    y, c = feat // NC, feat % NC

    def xdev(d):
        return (lax.rem(x + d + NX, NX) * NZ + z, feat)

    def zdev(d):
        return (x * NZ + lax.rem(z + d + NZ, NZ), feat)

    def fdev(dy, dc):
        return (row, lax.rem(y + dy, NY) * NC + lax.rem(c + dc, NC))

    plane_peers = sorted(
        ((dx, dz) for dx in range(NX) for dz in range(NZ) if (dx, dz) != (0, 0)),
        key=lambda d: -(min(d[0], NX - d[0]) + min(d[1], NZ - d[1])),
    )
    fcopies = [(dy, dc) for dy in (2, 1, 3, 0) for dc in range(NC) if (dy, dc) != (0, 0)]

    def xx(d):
        return lax.rem(x + d + NX, NX)

    def zz(d):
        return lax.rem(z + d + NZ, NZ)

    fcopy = pltpu.make_async_copy(fac, F, loc_sem.at[0])
    smalls = [
        pltpu.make_async_copy(w_hbm, w_ref, loc_sem.at[2]),
        pltpu.make_async_copy(st_hbm, st_ref, loc_sem.at[3]),
    ]
    mine = pltpu.make_async_copy(cand, G.at[x // 2, z, x % 2], loc_sem.at[1])
    mine.start()
    for cp in smalls:
        cp.start()
    fcopy.start()

    barrier = pltpu.get_barrier_semaphore()
    peers = [xdev(1), xdev(-1), zdev(1), zdev(-1), fdev(0, 1)] + [fdev(d, 0) for d in range(1, NY)]
    for dev in peers:
        pl.semaphore_signal(barrier, inc=1, device_id=dev, device_id_type=MESH)
    for cp in smalls:
        cp.wait()
    twice[0:1, 0:64] = w_ref[...]
    twice[0:1, 64:128] = w_ref[...]
    twice[1:2, 0:64] = st_ref[...].astype(jnp.float32)
    twice[1:2, 64:128] = st_ref[...].astype(jnp.float32)
    sub = lax.broadcasted_iota(jnp.int32, (NZ, 128), 0)
    lane = lax.broadcasted_iota(jnp.int32, (NZ, 128), 1)
    here = jnp.logical_and(sub == z, lane // 64 == x % 2)
    for k in range(2):
        placed = jnp.where(here, twice[k : k + 1, :], 0.0)
        for cp in range(2):
            wt[2 * k + cp] = jnp.where(x // 2 == cp, placed, 0.0)

    mine.wait()
    pl.semaphore_wait(barrier, len(peers))

    pending = []

    def remote(src, dst, ssem, rsem, dev, keep=True):
        cp = pltpu.make_async_remote_copy(
            src_ref=src, dst_ref=dst, send_sem=ssem, recv_sem=rsem, device_id=dev, device_id_type=MESH
        )
        cp.start()
        if keep:
            pending.append(cp)
        return cp

    count = [0]

    def gsend(view, dev):
        k = count[0]
        count[0] += 1
        return remote(view, view, gs.at[k], gr.at[k], dev)

    columns = cand.shape[1]
    rows_dev = cand.shape[0]
    half = rows_dev // 2

    def chunk(dx, dz, first, last, side=0):
        xp, zp = xx(dx), zz(dz)
        rows = {0: pl.ds(0, rows_dev), 1: pl.ds(0, half), -1: pl.ds(half, half)}[side]
        return G.at[xp // 2, zp, xp % 2, rows, pl.ds(first, last - first)]

    def own_column(o):
        if o == 0:
            return []
        return [(ZB, 4, 1), (ZB, 4, -1)] if o == 4 else [(ZB, abs(o), -1 if o > 0 else 1)]

    def message(kind, *at):
        if kind == XA1:
            (s,) = at
            return chunk(0, 0, 0, CUT_OWN), xdev(s), []
        if kind == XA2:
            (s,) = at
            return chunk(-s, 0, 0, CUT_OWN, s), xdev(s), [(XA1, s)]
        if kind == ZB:
            d, s = at
            side = s if d == 4 else 0
            return chunk(0, -s * (d - 1), CUT_NEXT, columns, side), zdev(s), [(ZB, d - 1, s)] if d > 1 else []
        if kind == XB:
            o, s = at
            return chunk(0, o, CUT_NEXT if o else CUT_OWN, columns), xdev(s), own_column(o)
        if kind == XH:
            o, s = at
            return chunk(-s, o, CUT_FAR if o else CUT_OWN, columns, s), xdev(s), [(XB, o, s)]
        d, s, r = at
        first = {0: [], 1: [(XA1, -1)], -1: [(XA1, 1)], 2: [(XA2, 1), (XA2, -1)]}[r]
        after = [(ZA, d - 1, s, r)] if d > 1 else first
        return chunk(r, -s * (d - 1), 0, CUT_FAR if r == 2 else CUT_NEXT), zdev(s), after

    def whole(o):
        keys = [(kind, o, s) for kind in (XB, XH) for s in (1, -1)] + own_column(o)
        if o == 0:
            return keys + [(kind, s) for kind in (XA1, XA2) for s in (1, -1)]
        if o == 4:
            return keys + [(ZA, 4, 1, 0), (ZA, 4, 1, 1), (ZA, 4, -1, 2), (ZA, 4, -1, -1)]
        return keys + [(ZA, abs(o), -1 if o > 0 else 1, r) for r in (0, 1, -1, 2)]

    sent, received = {}, set()

    def receive(keys):
        for key in keys:
            if key not in received:
                received.add(key)
                sent[key].wait_recv()

    def product(o):
        zp = zz(o)
        a = G[:, zp].reshape(NX * rows_dev, cand.shape[1])
        for n in range(2):
            rows = pl.ds(n * 256, 256)
            p = lax.dot_general(
                F[rows, :], a, (((1,), (1,)), ((), ())), preferred_element_type=jnp.float32
            ).astype(jnp.bfloat16)
            pb[zp, 0, rows, :] = p[:, :128]
            pb[zp, 1, rows, :] = p[:, 128:]

    PX, YS = {}, {}

    def send_half(o):
        i = OFFSETS.index(o)
        zp = zz(o)
        PX[o] = remote(pb.at[zp, 1 - c], px.at[zp], pxs.at[i], pxr.at[i], fdev(0, 1))

    def send_quarters(o):
        i = OFFSETS.index(o)
        zp = zz(o)
        PX[o].wait_recv()
        q = pb[zp, c].astype(jnp.float32) + px[zp].astype(jnp.float32)
        ysb[zp] = q.astype(jnp.bfloat16).reshape(NY, 128, 128)
        for d in (2, 1, 3):
            yp = lax.rem(y + d, NY)
            YS[o, d] = remote(
                ysb.at[zp, yp], ysr.at[zp, d], yss.at[i * 3 + d - 1], ysrs.at[i * 3 + d - 1], fdev(d, 0)
            )

    def squares(o):
        zp = zz(o)
        total = ysb[zp, y].astype(jnp.float32)
        for d in range(1, NY):
            YS[o, d].wait_recv()
            total = total + ysr[zp, d].astype(jnp.float32)
        V[pl.ds(zp, 1), :] = jnp.sum(total * total, axis=0, keepdims=True)

    block = Ci.shape[-1]
    col0 = pl.multiple_of((z % 4) * block, block)
    croot = z // 4
    dy = lax.rem(y - x + NY, NY)
    on_core = c == croot
    is_root = jnp.logical_and(dy == 0, on_core)

    def ci_copy(o, slot, src, dev):
        i = OFFSETS.index(o)
        return pltpu.make_async_remote_copy(
            src_ref=src, dst_ref=Ci.at[:, zz(o)], send_sem=cs.at[i * 3 + slot], recv_sem=cr.at[i],
            device_id=dev, device_id_type=MESH,
        )

    def ci_source(o):
        return G.at[:, zz(o), :, :, pl.ds(col0, block)]

    def ci_root(o):
        @pl.when(is_root)
        def _():
            src = ci_source(o)
            ci_copy(o, 0, src, fdev(1, 0)).start()
            ci_copy(o, 1, src, fdev(3, 0)).start()
            ci_copy(o, 2, src, fdev(0, 1)).start()
            own = pltpu.make_async_copy(src, Ci.at[:, zz(o)], cr.at[OFFSETS.index(o)])
            own.start()
            own.wait()

    def ci_wait(o):
        ci_copy(o, 0, Ci.at[:, zz(o)], fdev(0, 1)).wait_recv()

    def ci_near(o):
        i = OFFSETS.index(o)
        for d in (1, 3):
            @pl.when(jnp.logical_and(on_core, dy == d))
            def _():
                ci_wait(o)
                if d == (1 if i % 2 == 0 else 3):
                    ci_copy(o, 0, Ci.at[:, zz(o)], fdev(d, 0)).start()
                ci_copy(o, 2, Ci.at[:, zz(o)], fdev(0, 1)).start()

    def ci_far(o):
        @pl.when(jnp.logical_and(on_core, dy == 2))
        def _():
            ci_wait(o)
            ci_copy(o, 2, Ci.at[:, zz(o)], fdev(0, 1)).start()

    def ci_last(o):
        @pl.when(jnp.logical_not(on_core))
        def _():
            ci_wait(o)

        for cp in range(2):
            t = Ci[cp, zz(o)].reshape(128, block)
            S[:, pl.ds(pl.multiple_of((cp * NZ + zz(o)) * 128, 128), 128)] = t.T

    def ci_finish(o):
        i = OFFSETS.index(o)

        @pl.when(is_root)
        def _():
            for slot in range(3):
                ci_copy(o, slot, ci_source(o), fdev(0, 1)).wait_send()

        for d in (1, 2, 3):
            @pl.when(jnp.logical_and(on_core, dy == d))
            def _():
                if d == (1 if i % 2 == 0 else 3):
                    ci_copy(o, 0, Ci.at[:, zz(o)], fdev(0, 1)).wait_send()
                ci_copy(o, 2, Ci.at[:, zz(o)], fdev(0, 1)).wait_send()

    WX, WZ = [], []
    near, far = [], []
    for op in ORDER:
        kind, at = op[0], op[1:]
        if kind <= ZA:
            view, dev, after = message(*op)
            receive(after)
            sent[op] = gsend(view, dev)
        elif kind == PRODUCT:
            (o,) = at
            receive(whole(o))
            if o == 0:
                fcopy.wait()
            if o != 4:
                ci_root(o)
            product(o)
            send_half(o)
            if o == 0:
                WX = [remote(wt, wx.at[d], ws.at[d - 1], wr.at[d - 1], xdev(d)) for d in range(1, NX)]
            if o == -2:
                total = wt[...]
                for d in range(1, NX):
                    WX[d - 1].wait_recv()
                    total = total + wx[d]
                wz0[...] = total
                receive(own_column(4))
                WZ = [remote(wz0, wz.at[d], ws.at[d + 2], wr.at[d + 2], zdev(d)) for d in range(1, NZ)]
        elif kind == QUARTERS:
            send_quarters(*at)
            if at == (4,):
                ci_root(4)
                for o in OFFSETS[:-1]:
                    if o not in near:
                        ci_near(o)
                        near.append(o)
                last = list(far)
                for o in last:
                    ci_last(o)
        elif kind == SQUARES:
            squares(*at)
        elif kind == NEAR:
            ci_near(*at)
            near += at
        else:
            ci_far(*at)
            far += at

    lz0[...] = V[...]
    for k, (dx, dz) in enumerate(plane_peers):
        remote(lz0, lz.at[k], ls.at[0], lr.at[0], (xx(dx) * NZ + zz(dz), feat), keep=False)
    all_sums = pltpu.make_async_remote_copy(
        src_ref=lz, dst_ref=lz, send_sem=ls.at[0], recv_sem=lr.at[0], device_id=xdev(1), device_id_type=MESH
    )
    ci_near(4)
    for o in OFFSETS[:-1]:
        if o not in far:
            ci_far(o)
            far.append(o)
    total = wz0[...]
    for d in range(1, NZ):
        WZ[d - 1].wait_recv()
        total = total + wz[d]
    weights, labels = [total[0], total[1]], [total[2], total[3]]
    ids = lax.broadcasted_iota(jnp.int32, (STRATA, 128), 0).astype(jnp.float32)

    def over_strata(tiles):
        acc = jnp.zeros((STRATA, 128), jnp.float32)
        for cp in range(2):
            for zp in range(NZ):
                acc = acc + jnp.where(labels[cp][zp : zp + 1, :] == ids, tiles[cp][zp : zp + 1, :], 0.0)
        return jnp.sum(acc, axis=1, keepdims=True)

    mass = over_strata(weights)
    for cp in pending:
        cp.wait_send()
    late = OFFSETS[-3:]
    for o in OFFSETS:
        if o not in last and o not in late:
            ci_last(o)
    v = lz0[...]
    all_sums.wait_recv()
    for k in range(len(plane_peers)):
        v = v + lz[k]
    lt0[...] = v
    LT = [
        remote(lt0, lt.at[k], ls.at[k + 9], lr.at[k + 9], fdev(*d), keep=False)
        for k, d in enumerate(fcopies, 1)
    ]
    all_sums.wait_send()
    ci_far(4)
    for o in late:
        ci_last(o)
    for o in OFFSETS:
        ci_finish(o)
    same, other = lt0[...], None
    for k, (dyk, dck) in enumerate(fcopies, 1):
        LT[k - 1].wait_recv()
        if dck == 0:
            same = same + lt[k]
        else:
            other = lt[k] if other is None else other + lt[k]
    first = c == 0
    raw = [jnp.where(first, same, other), jnp.where(first, other, same)]
    products = [weights[cp] * raw[cp] for cp in range(2)]
    ratio = mass / over_strata(products)
    new_weights = []
    for cp in range(2):
        rows = [
            jnp.sum(jnp.where(labels[cp][zp : zp + 1, :] == ids, ratio, 0.0), axis=0, keepdims=True)
            for zp in range(NZ)
        ]
        row_ratio = jnp.concatenate(rows, axis=0)
        new_weight = products[cp] * row_ratio
        new_weights.append(new_weight)
        step = new_weight - weights[cp]
        for zp in range(NZ):
            cols = pl.ds((cp * NZ + zp) * 128, 128)
            S[:, cols] = (S[:, cols].astype(jnp.float32) * step[zp : zp + 1, :]).astype(jnp.bfloat16)

    def own_rows(tiles):
        tile = jnp.where(x // 2 == 0, tiles[0], tiles[1])
        line = jnp.sum(jnp.where(sub == z, tile, 0.0), axis=0, keepdims=True)
        return jnp.where(x % 2 == 0, line[:, :64], line[:, 64:])

    nw_ref[...] = own_rows(new_weights)
    lev_ref[...] = own_rows(raw) / features
    for cp in LT:
        cp.wait_send()


def gather(cand, fac, weights, strata):
    rows_dev, feat_block = cand.shape
    row_block = fac.shape[0]
    bf, f32 = jnp.bfloat16, jnp.float32
    vmem = pl.BlockSpec(memory_space=pltpu.VMEM)
    hbm = pl.BlockSpec(memory_space=pltpu.HBM)
    dma = pltpu.SemaphoreType.DMA
    return pl.pallas_call(
        gather_kernel,
        out_shape=(
            pltpu.VMEM((2, NZ, 2, rows_dev, feat_block), bf),
            pltpu.VMEM((row_block, NX * NZ * rows_dev), bf),
            pltpu.VMEM((1, rows_dev), f32),
            pltpu.VMEM((1, rows_dev), f32),
        ),
        in_specs=[hbm, hbm, hbm, hbm],
        out_specs=(vmem, vmem, vmem, vmem),
        scratch_shapes=[
            pltpu.VMEM((1, rows_dev), f32),
            pltpu.VMEM((1, rows_dev), jnp.int32),
            pltpu.VMEM((8, 128), f32),
            pltpu.VMEM((4, NZ, 128), f32),
            pltpu.VMEM(fac.shape, bf),
            pltpu.VMEM((2, NZ, 2, rows_dev, row_block), bf),
            pltpu.VMEM((NZ, 2, row_block, 128), bf),
            pltpu.VMEM((NZ, row_block, 128), bf),
            pltpu.VMEM((NZ, NY, 128, 128), bf),
            pltpu.VMEM((NZ, NY, 128, 128), bf),
            pltpu.VMEM((NZ, 128), f32),
            pltpu.VMEM((NX, 4, NZ, 128), f32),
            pltpu.VMEM((4, NZ, 128), f32),
            pltpu.VMEM((NZ, 4, NZ, 128), f32),
            pltpu.VMEM((NZ, 128), f32),
            pltpu.VMEM((NX * NZ - 1, NZ, 128), f32),
            pltpu.VMEM((NZ, 128), f32),
            pltpu.VMEM((NZ, NZ, 128), f32),
            dma((4,)),
            dma((72,)),
            dma((72,)),
            dma((10,)),
            dma((10,)),
            dma((8,)),
            dma((8,)),
            dma((24,)),
            dma((24,)),
            dma((24,)),
            dma((8,)),
            dma((17,)),
            dma((17,)),
        ],
        compiler_params=pltpu.CompilerParams(
            collective_id=0, has_side_effects=True, vmem_limit_bytes=40 * 1024 * 1024
        ),
    )(*[
        pltpu.with_memory_space_constraint(a, pltpu.HBM)
        for a in (cand, fac, weights.reshape(1, rows_dev), strata.reshape(1, rows_dev))
    ])


WIDTH = 512


def increment_kernel(s_ref, g_ref, nw_ref, lev_ref, o_hbm, nw_hbm, lev_hbm, out, sem):
    copies = [
        pltpu.make_async_copy(nw_ref, nw_hbm, sem.at[0]),
        pltpu.make_async_copy(lev_ref, lev_hbm, sem.at[1]),
    ]
    for cp in copies:
        cp.start()
    for j in range(out.shape[1] // WIDTH):
        cols = pl.ds(j * WIDTH, WIDTH)
        out[:, cols] = jnp.dot(s_ref[...], g_ref[:, cols], preferred_element_type=jnp.float32)
        cp = pltpu.make_async_copy(out.at[:, cols], o_hbm.at[:, cols], sem.at[2 + j])
        cp.start()
        copies.append(cp)
    for cp in copies:
        cp.wait()


def increment(s, g, nw, lev):
    rows = s.shape[0]
    columns = g.shape[1]
    vmem = pl.BlockSpec(memory_space=pltpu.VMEM)
    hbm = pl.BlockSpec(memory_space=pltpu.HBM)
    f32 = jnp.float32
    return pl.pallas_call(
        increment_kernel,
        out_shape=(pltpu.HBM((rows, columns), f32), pltpu.HBM(nw.shape, f32), pltpu.HBM(lev.shape, f32)),
        in_specs=[vmem] * 4,
        out_specs=(hbm,) * 3,
        scratch_shapes=[
            pltpu.VMEM((rows, columns), f32),
            pltpu.SemaphoreType.DMA((2 + columns // WIDTH,)),
        ],
        compiler_params=pltpu.CompilerParams(vmem_limit_bytes=30 * 1024 * 1024),
    )(s, g, nw, lev)


def per_device(candidates, inv_factor, weights, strata):
    g, s, nw, lev = gather(candidates, inv_factor, weights, strata)
    information, nw, lev = increment(s, g.reshape(-1, g.shape[-1]), nw, lev)
    return (nw.reshape(weights.shape), lev.reshape(weights.shape), information)


def solution(mesh):
    in_specs = (P("row", "feat"), P("row", "feat"), P("row"), P("row"))
    out_specs = (P("row"), P("row"), P("row", "feat"))
    return jax.shard_map(
        per_device, mesh=mesh, in_specs=in_specs, out_specs=out_specs, check_vma=False
    )
```
